512 devices in a mesh: lat: 64 (over y, x, z_hi, core), lev: 8 (over z_lo).
Axes of the slice: x: 4, y: 4, z: 16 (z_hi: 2, z_lo: 8; z = z_hi * 8 + z_lo), core: 2. Of those that a mesh axis runs over, the one named last changes fastest.
Arguments:
- spectral: bfloat16 [8, 16, 2, 320, 320], P(None, 'lev', None, 'lat'), may hold values from -0.009765625 to 0.009765625
- legendre: bfloat16 [320, 320, 320], P('lat'), may hold values from -6 to 6
- quad_weight: float32 [320], replicated, may hold values from 1 to 4
- w_in: bfloat16 [128, 256], replicated, may hold values from -0.5 to 0.5
- b_in: float32 [256], replicated, may hold values from -3 to 3
- w_out: bfloat16 [256, 128], replicated, may hold values from -0.375 to 0.375
- b_out: float32 [128], replicated, may hold values from -3 to 3
Outputs:
- tendency_spec: float32 [8, 16, 2, 320, 320], P(None, 'lev', None, 'lat')
The draws below stay inside these ranges and needn't reach their ends.
All inputs are finite; a program needn't handle non-finite values.
Results may differ from the reference program's by a relative error of at most 0.0055.
Values may be sent and summed in bfloat16 or wider, within the bound.
A program may use at most 64 MiB of HBM per device.

```python
import math
import jax
import jax.numpy as jnp
from jax import lax

M = 320
N = 320
NLON = 1280
F = 8
LEVELS = 16
HID = 256
FEAT = 128
HALF = 320


def level_of(key, extent, cuts, smallest, largest):
    gain, own = 1.0, jax.random.fold_in(key, 6)
    for dim, shards_of in cuts:
        heights = jnp.exp(jax.random.uniform(jax.random.fold_in(own, dim), (shards_of,), jnp.float32, smallest / len(cuts), largest / len(cuts)))
        gain = gain * jnp.repeat(heights, extent[dim] // shards_of).reshape([-1 if axis == dim else 1 for axis in range(len(extent))])
    return gain


def centred(rng, dims, width, most, shards=(), kind=jnp.bfloat16):
    entries = width * jax.random.normal(rng, dims, jnp.float32)
    if shards:
        entries = entries * level_of(rng, dims, shards, -0.22, 0.18)
    return jnp.clip(entries, -most, most).astype(kind)


def setup_inputs(seed: int = 0) -> dict:
    splits = jax.random.split(jax.random.key(seed), 8)
    return {
        "spectral": centred(splits[0], (F, LEVELS, 2, M, N), (4 * M * N) ** -0.5, 0.009765625, ((1, 8), (3, 64))),
        "legendre": centred(splits[1], (M, N, HALF), 1.0, 6.0, ((0, 64),)),
        "quad_weight": jnp.clip(jnp.exp(jax.random.uniform(splits[2], (HALF,), jnp.float32, math.log(1.0), math.log(4.0))), 1.0, 4.0),
        "w_in": centred(splits[3], (FEAT, HID), FEAT ** -0.5, 0.5),
        "b_in": centred(splits[4], (HID,), 0.5, 3.0, (), jnp.float32),
        "w_out": centred(splits[5], (HID, FEAT), HID ** -0.5, 0.375),
        "b_out": centred(splits[6], (FEAT,), 0.5, 3.0, (), jnp.float32),
    }


def fourier_tables(wave_count, lon_count):
    wavenumbers = jnp.arange(wave_count, dtype=jnp.int32)
    longitudes = jnp.arange(lon_count, dtype=jnp.int32)
    phases = (wavenumbers[:, None] * longitudes[None, :]) % lon_count
    angles = phases.astype(jnp.float32) * (2.0 * math.pi / lon_count)
    cosines = jnp.cos(angles)
    sines = jnp.sin(angles)
    factors = jnp.where(wavenumbers == 0, 1.0, 2.0).astype(jnp.float32)[:, None]
    inverse = jnp.concatenate([factors * cosines, -factors * sines], axis=0).astype(jnp.bfloat16)
    forward = (jnp.concatenate([cosines, -sines], axis=0).T / lon_count).astype(jnp.bfloat16)
    return inverse, forward


def reference(spectral, legendre, quad_weight, w_in, b_in, w_out, b_out):
    parity = jnp.where(jnp.arange(N, dtype=jnp.int32) % 2 == 0, 1.0, -1.0).astype(jnp.bfloat16)
    mirrored = (legendre * parity[None, :, None])[:, :, ::-1]
    full_table = jnp.concatenate([legendre, mirrored], axis=2)
    coefficients = spectral.reshape(FEAT, 2, M, N).astype(jnp.float32)
    fourier = jnp.einsum("crmn,mnl->lcrm", coefficients, full_table.astype(jnp.float32)).astype(jnp.bfloat16)
    inverse, forward = fourier_tables(M, NLON)

    def one_row(lat_row):
        grid_values = jnp.dot(lat_row.reshape(FEAT, 2 * M), inverse, preferred_element_type=jnp.float32).astype(jnp.bfloat16)
        hidden = jnp.dot(w_in.T, grid_values, preferred_element_type=jnp.float32) + b_in[:, None]
        hidden = jax.nn.gelu(hidden).astype(jnp.bfloat16)
        tendency = (jnp.dot(w_out.T, hidden, preferred_element_type=jnp.float32) + b_out[:, None]).astype(jnp.bfloat16)
        row_coeffs = jnp.dot(tendency, forward, preferred_element_type=jnp.float32).astype(jnp.bfloat16)
        return row_coeffs.reshape(FEAT, 2, M)

    coeffs = lax.map(one_row, fourier)
    northern = coeffs[:HALF].astype(jnp.float32)
    southern = coeffs[HALF:][::-1].astype(jnp.float32)
    weighting = quad_weight[:, None, None, None]
    even_part = ((northern + southern) * weighting).astype(jnp.bfloat16)
    odd_part = ((northern - southern) * weighting).astype(jnp.bfloat16)
    out_even = jnp.einsum("jcrm,mnj->crmn", even_part.astype(jnp.float32), legendre[:, 0::2].astype(jnp.float32))
    out_odd = jnp.einsum("jcrm,mnj->crmn", odd_part.astype(jnp.float32), legendre[:, 1::2].astype(jnp.float32))
    result = jnp.stack([out_even, out_odd], axis=-1).reshape(FEAT, 2, M, N)
    return result.reshape(F, LEVELS, 2, M, N)
```

```python
import functools
import math

import jax
import jax.numpy as jnp
import ml_dtypes
import numpy as np
from jax import lax
from jax.experimental import pallas as pl
from jax.experimental.pallas import tpu as pltpu
from jax.sharding import PartitionSpec as P

MESH = pl.DeviceIdType.MESH
NLON = 1280
WAVES = 320
ZN = 16
PN = 32
SLOTS = 10
OWN_M = 5
KP = 24


def tables():
    m = np.arange(WAVES, dtype=np.int64)
    x = np.arange(NLON, dtype=np.int64)
    angle = ((m[:, None] * x[None, :]) % NLON).astype(np.float32) * np.float32(2.0 * math.pi / NLON)
    cosines, sines = np.cos(angle), np.sin(angle)
    factor = np.where(m == 0, 1.0, 2.0).astype(np.float32)[:, None]
    inverse = np.stack([factor * cosines, -factor * sines], axis=1)
    forward = np.stack([cosines, -sines], axis=1) / np.float32(NLON)

    def arrange(table):
        t = table.reshape(16, 2, 2, OWN_M, 2, NLON).transpose(0, 2, 1, 3, 4, 5).reshape(PN, 4 * OWN_M, NLON)
        padded = np.zeros((PN, KP, NLON), np.float32)
        padded[:, : 4 * OWN_M] = t
        return padded.reshape(PN * KP, NLON).astype(ml_dtypes.bfloat16)

    return np.ascontiguousarray(arrange(inverse).T), arrange(forward)


def device(plane_index, z):
    return {"lat": (plane_index // 2) * 4 + (z // 8) * 2 + plane_index % 2, "lev": z % 8}


def slot_of(z):
    s = (5 * z + 7) // 8
    return s, (8 * s) // 5 == z


def far_first(k):
    return jnp.where(k % 2 == 1, 8 - k // 2, 8 + k // 2)


def kernel(
    spec_ref, leg_hbm, qw_ref, w_in_ref, b_in_ref, w_out_ref, b_out_ref, tinv_hbm, tfwd_hbm,
    out_ref,
    leg, tinv, tfwd, spec32, zsend, zrecv, rows32, psend, precv, tend, bsend, brecv, zbsend, zbrecv,
    load_sem, zs_sem, zr_sem, ps_sem, pr_sem, bs_sem, br_sem, zbs_sem, zbr_sem,
):
    lat = lax.axis_index("lat")
    z = ((lat // 2) % 2) * 8 + lax.axis_index("lev")
    me = (lat // 4) * 2 + lat % 2
    slot, active = slot_of(z)

    leg_load = pltpu.make_async_copy(leg_hbm, leg, load_sem.at[0])
    tinv_load = pltpu.make_async_copy(tinv_hbm, tinv, load_sem.at[1])
    tfwd_load = pltpu.make_async_copy(tfwd_hbm, tfwd, load_sem.at[2])
    leg_load.start()

    barrier = pltpu.get_barrier_semaphore()

    def greet_z(k, carry):
        other = (z + k) % ZN
        _, other_active = slot_of(other)

        @pl.when(jnp.logical_or(active, other_active))
        def _():
            pl.semaphore_signal(barrier, inc=1, device_id=device(me, other), device_id_type=MESH)

        return carry

    lax.fori_loop(1, ZN, greet_z, 0)

    @pl.when(active)
    def _():
        def greet_plane(k, carry):
            pl.semaphore_signal(barrier, inc=1, device_id=device((me + k) % PN, z), device_id_type=MESH)
            return carry

        lax.fori_loop(1, PN, greet_plane, 0)
        tinv_load.start()
        tfwd_load.start()

    for c in range(32):
        values = spec_ref[c].astype(jnp.float32)
        for b, width in enumerate((128, 128, 64)):
            spec32[b, pl.ds(c * 8, OWN_M), 0:width] = values[:, 128 * b : 128 * b + width]
    lane = lax.broadcasted_iota(jnp.int32, (1, WAVES), 1)
    even_lane = lane % 2 == 0
    leg_load.wait()
    for m in range(OWN_M):
        real = jnp.concatenate([spec32[b, pl.ds(m, 16, stride=16), :] for b in range(3)], axis=1)
        imag = jnp.concatenate([spec32[b, pl.ds(8 + m, 16, stride=16), :] for b in range(3)], axis=1)
        both = jnp.concatenate([real, imag], axis=0)[:, :WAVES]
        lhs = jnp.concatenate([jnp.where(even_lane, both, 0.0), jnp.where(even_lane, 0.0, both)], axis=0)
        sums = jnp.dot(lhs.astype(jnp.bfloat16), leg[m], preferred_element_type=jnp.float32)
        north = sums[:32] + sums[32:]
        south = sums[:32] - sums[32:]
        for s in range(SLOTS):
            cols = slice(32 * s, 32 * s + 32)
            piece = jnp.concatenate([north[:16, cols], south[:16, cols], north[16:, cols], south[16:, cols]], axis=1)
            zsend[s, m * 16 : (m + 1) * 16, :] = piece.astype(jnp.bfloat16)

    @pl.when(active)
    def _():
        pl.semaphore_wait(barrier, ZN - 1 + PN - 1)

    @pl.when(jnp.logical_not(active))
    def _():
        pl.semaphore_wait(barrier, SLOTS)

    def send_z(k, carry):
        other = (z + far_first(k)) % ZN
        s, ok = slot_of(other)

        @pl.when(ok)
        def _():
            pltpu.make_async_remote_copy(
                zsend.at[s], zrecv.at[z], zs_sem, zr_sem, device_id=device(me, other), device_id_type=MESH
            ).start()

        return carry

    lax.fori_loop(1, ZN, send_z, 0)

    @pl.when(active)
    def _():
        pltpu.make_async_copy(zsend.at[slot], zrecv.at[z], zr_sem).start()
        pad = jnp.zeros((PN, 128), jnp.float32)
        for hemi in range(2):
            for k in range(20, KP):
                rows32[pl.ds(hemi * KP + k, PN, stride=2 * KP), :] = pad

        row = lax.broadcasted_iota(jnp.int32, (128, 128), 0)
        col = lax.broadcasted_iota(jnp.int32, (128, 128), 1)
        wanted = ((row % 16) // 2) * 16 + (row // 16) * 2 + row % 2
        onehot32 = jnp.where(col == wanted, 1.0, 0.0).astype(jnp.float32)
        onehot = onehot32.astype(jnp.bfloat16)
        eye32 = jnp.where(row == col, 1.0, 0.0).astype(jnp.float32)
        w_in = jnp.dot(onehot, w_in_ref[...], preferred_element_type=jnp.float32).astype(jnp.bfloat16)
        w_out = lax.dot_general(
            w_out_ref[...], onehot, (((1,), (1,)), ((), ())), preferred_element_type=jnp.float32
        ).astype(jnp.bfloat16)
        b_col = jnp.sum(onehot32 * b_out_ref[...], axis=1, keepdims=True)
        b_out = jnp.sum(eye32 * b_col, axis=0, keepdims=True)
        b_in = b_in_ref[...]

        pltpu.make_async_copy(zrecv, zrecv, zr_sem).wait()

        for half in range(2):
            for m in range(OWN_M):
                block = jnp.concatenate(
                    [zrecv[half * 8 + g, m * 16 : (m + 1) * 16, :] for g in range(8)], axis=0
                ).astype(jnp.float32)
                turned = block.T
                for r in range(2):
                    for hemi in range(2):
                        q = (r * 2 + hemi) * 32
                        k = hemi * KP + (half * OWN_M + m) * 2 + r
                        rows32[pl.ds(k, PN, stride=2 * KP), :] = turned[q : q + 32]
        psend[...] = rows32[...].reshape(PN, 2 * KP, 128).astype(jnp.bfloat16)

        def send_plane(k, carry):
            other = (me + k) % PN
            pltpu.make_async_remote_copy(
                psend.at[other], precv.at[me], ps_sem, pr_sem, device_id=device(other, z), device_id_type=MESH
            ).start()
            return carry

        lax.fori_loop(1, PN, send_plane, 0)
        pltpu.make_async_copy(psend.at[me], precv.at[me], pr_sem).start()
        tinv_load.wait()
        tfwd_load.wait()
        pltpu.make_async_copy(precv, precv, pr_sem).wait()

        got = precv[...].astype(jnp.float32)
        waves = jnp.concatenate(
            [got[:, :KP].reshape(PN * KP, 128).astype(jnp.bfloat16), got[:, KP:].reshape(PN * KP, 128).astype(jnp.bfloat16)],
            axis=1,
        )
        tile = 256

        def columns(i, carry):
            rows = pl.ds(pl.multiple_of(i * tile, tile), tile)
            grid = jnp.dot(tinv[rows, :], waves, preferred_element_type=jnp.float32).astype(jnp.bfloat16)
            for hemi in range(2):
                part = slice(hemi * 128, hemi * 128 + 128)
                hidden = jnp.dot(grid[:, part], w_in, preferred_element_type=jnp.float32) + b_in
                hidden = jax.nn.gelu(hidden).astype(jnp.bfloat16)
                value = jnp.dot(hidden, w_out, preferred_element_type=jnp.float32) + b_out
                tend[rows, part] = value.astype(jnp.bfloat16)
            return carry

        lax.fori_loop(0, NLON // tile, columns, 0)
        weight = qw_ref[slot * 32 + me]

        def back(i, carry):
            rows = pl.ds(pl.multiple_of(i * 8 * KP, 8 * KP), 8 * KP)
            coeffs = jnp.dot(tfwd[rows, :], tend[...], preferred_element_type=jnp.float32)
            coeffs = coeffs.astype(jnp.bfloat16).astype(jnp.float32)
            north, south = coeffs[:, :128], coeffs[:, 128:]
            even = ((north + south) * weight).reshape(8, KP, 128)
            odd = ((north - south) * weight).reshape(8, KP, 128)
            bsend[pl.ds(i * 8, 8)] = jnp.concatenate([even, odd], axis=1).astype(jnp.bfloat16)
            return carry

        lax.fori_loop(0, PN // 8, back, 0)

        def return_plane(k, carry):
            other = (me + k) % PN
            pltpu.make_async_remote_copy(
                bsend.at[other], brecv.at[me], bs_sem, br_sem, device_id=device(other, z), device_id_type=MESH
            ).start()
            return carry

        lax.fori_loop(1, PN, return_plane, 0)
        pltpu.make_async_copy(bsend.at[me], brecv.at[me], br_sem).start()
        pltpu.make_async_copy(brecv, brecv, br_sem).wait()

        rows32[...] = brecv[...].astype(jnp.float32).reshape(PN * 2 * KP, 128)
        for half in range(2):
            for m in range(OWN_M):
                blocks = []
                for r in range(2):
                    for par in range(2):
                        k = par * KP + (half * OWN_M + m) * 2 + r
                        blocks.append(rows32[pl.ds(k, PN, stride=2 * KP), :])
                turned = jnp.concatenate(blocks, axis=0).T.astype(jnp.bfloat16)
                for g in range(8):
                    zbsend[half * 8 + g, m * 16 : (m + 1) * 16, :] = turned[g * 16 : (g + 1) * 16]

        def return_z(k, carry):
            other = (z + far_first(k)) % ZN
            pltpu.make_async_remote_copy(
                zbsend.at[other], zbrecv.at[slot], zbs_sem, zbr_sem, device_id=device(me, other), device_id_type=MESH
            ).start()
            return carry

        lax.fori_loop(1, ZN, return_z, 0)
        pltpu.make_async_copy(zbsend.at[z], zbrecv.at[slot], zbr_sem).start()

    pltpu.make_async_copy(zbrecv, zbrecv, zbr_sem).wait()

    for m in range(OWN_M):
        parts = []
        for par in range(2):
            for r in range(2):
                q = (r * 2 + par) * 32
                parts.append(
                    jnp.concatenate(
                        [zbrecv[s, m * 16 : (m + 1) * 16, :].astype(jnp.float32)[:, q : q + 32] for s in range(SLOTS)],
                        axis=1,
                    )
                )
        lhs = jnp.concatenate(parts, axis=0).astype(jnp.bfloat16)
        sums = lax.dot_general(lhs, leg[m], (((1,), (1,)), ((), ())), preferred_element_type=jnp.float32)
        result = jnp.where(even_lane, sums[:32], sums[32:])
        result = jnp.concatenate([result, jnp.zeros((32, 64), jnp.float32)], axis=1)
        for b in range(3):
            cols = slice(128 * b, 128 * b + 128)
            spec32[b, pl.ds(m, 16, stride=16), :] = result[:16, cols]
            spec32[b, pl.ds(8 + m, 16, stride=16), :] = result[16:, cols]
    for c in range(32):
        for b, width in enumerate((128, 128, 64)):
            out_ref[c, :, 128 * b : 128 * b + width] = spec32[b, pl.ds(c * 8, OWN_M), 0:width]

    @pl.when(active)
    def _():
        pltpu.make_async_copy(zsend.at[0:9], zsend.at[0:9], zs_sem).wait()
        pltpu.make_async_copy(psend.at[0:31], psend.at[0:31], ps_sem).wait()
        pltpu.make_async_copy(bsend.at[0:31], bsend.at[0:31], bs_sem).wait()
        pltpu.make_async_copy(zbsend.at[0:15], zbsend.at[0:15], zbs_sem).wait()

    @pl.when(jnp.logical_not(active))
    def _():
        pltpu.make_async_copy(zsend, zsend, zs_sem).wait()


def shards(tinv, tfwd, spectral, legendre, quad_weight, w_in, b_in, w_out, b_out):
    bf16, f32 = jnp.bfloat16, jnp.float32
    vmem, hbm, smem = (pl.BlockSpec(memory_space=s) for s in (pltpu.VMEM, pl.ANY, pltpu.SMEM))
    out = pl.pallas_call(
        kernel,
        out_shape=jax.ShapeDtypeStruct((32, OWN_M, WAVES), f32),
        in_specs=[vmem, hbm, smem, vmem, vmem, vmem, vmem, hbm, hbm],
        out_specs=vmem,
        scratch_shapes=[
            pltpu.VMEM(legendre.shape, bf16),
            pltpu.VMEM((NLON, PN * KP), bf16),
            pltpu.VMEM((PN * KP, NLON), bf16),
            pltpu.VMEM((3, 256, 128), f32),
            pltpu.VMEM((SLOTS, 80, 128), bf16),
            pltpu.VMEM((ZN, 80, 128), bf16),
            pltpu.VMEM((PN * 2 * KP, 128), f32),
            pltpu.VMEM((PN, 2 * KP, 128), bf16),
            pltpu.VMEM((PN, 2 * KP, 128), bf16),
            pltpu.VMEM((NLON, 256), bf16),
            pltpu.VMEM((PN, 2 * KP, 128), bf16),
            pltpu.VMEM((PN, 2 * KP, 128), bf16),
            pltpu.VMEM((ZN, 80, 128), bf16),
            pltpu.VMEM((SLOTS, 80, 128), bf16),
            pltpu.SemaphoreType.DMA((3,)),
        ]
        + [pltpu.SemaphoreType.DMA] * 8,
        compiler_params=pltpu.CompilerParams(collective_id=0, has_side_effects=True, vmem_limit_bytes=48 << 20),
        name="transform_step",
    )(
        spectral.reshape(32, OWN_M, WAVES), legendre, quad_weight,
        w_in, b_in.reshape(1, -1), w_out, b_out.reshape(1, -1), tinv, tfwd,
    )
    return out.reshape(spectral.shape)


def solution(mesh):
    tinv, tfwd = tables()
    in_specs = (P(), P(), P(None, "lev", None, "lat", None), P("lat", None, None), P(), P(), P(), P(), P())
    out_specs = P(None, "lev", None, "lat", None)
    step = jax.shard_map(shards, mesh=mesh, in_specs=in_specs, out_specs=out_specs, check_vma=False)
    return lambda *args: step(jnp.asarray(tinv), jnp.asarray(tfwd), *args)
```

```python
import functools
import math

import jax
import jax.numpy as jnp
import ml_dtypes
import numpy as np
from jax import lax
from jax.experimental import pallas as pl
from jax.experimental.pallas import tpu as pltpu
from jax.sharding import PartitionSpec as P

MESH = pl.DeviceIdType.MESH
NLON = 1280
WAVES = 320
ZN = 16
PN = 32
SLOTS = 10
OWN_M = 5
TILE = 320
KP = 24


def tables():
    m = np.arange(WAVES, dtype=np.int64)
    x = np.arange(NLON, dtype=np.int64)
    angle = ((m[:, None] * x[None, :]) % NLON).astype(np.float32) * np.float32(2.0 * math.pi / NLON)
    cosines, sines = np.cos(angle), np.sin(angle)
    factor = np.where(m == 0, 1.0, 2.0).astype(np.float32)[:, None]
    inverse = np.stack([factor * cosines, -factor * sines], axis=1)
    forward = np.stack([cosines, -sines], axis=1) / np.float32(NLON)

    def arrange(table):
        t = table.reshape(16, 2, 2, OWN_M, 2, NLON).transpose(0, 2, 1, 3, 4, 5).reshape(PN, 4 * OWN_M, NLON)
        padded = np.zeros((PN, KP, NLON), np.float32)
        padded[:, : 4 * OWN_M] = t
        return padded.reshape(PN * KP, NLON).astype(ml_dtypes.bfloat16)

    return np.ascontiguousarray(arrange(inverse).T), arrange(forward)


def device(plane_index, z):
    return {"lat": (plane_index // 2) * 4 + (z // 8) * 2 + plane_index % 2, "lev": z % 8}


def slot_of(z):
    s = (5 * z + 7) // 8
    return s, (8 * s) // 5 == z


def far_first(k):
    return jnp.where(k % 2 == 1, 8 - k // 2, 8 + k // 2)


def kernel(
    spec_hbm, leg_hbm, qw_hbm, w_in_hbm, b_in_hbm, w_out_hbm, b_out_hbm, tinv_hbm, tfwd_hbm,
    out_ref,
    spec_ref, leg, qw_ref, w_in_ref, b_in_ref, w_out_ref, b_out_ref, tinv, tfwd, spec32, zsend, zrecv, rows32, psend, precv, tend, bsend, brecv, zbsend, zbrecv,
    load_sem, zs_sem, zr_sem, ps_sem, pr_sem, bs_sem, br_sem, zbs_sem, zbr_sem,
):
    lat = lax.axis_index("lat")
    z = ((lat // 2) % 2) * 8 + lax.axis_index("lev")
    me = (lat // 4) * 2 + lat % 2
    slot, active = slot_of(z)

    spec_load = pltpu.make_async_copy(spec_hbm, spec_ref, load_sem.at[0])
    leg_load = pltpu.make_async_copy(leg_hbm, leg, load_sem.at[1])
    weight_load = pltpu.make_async_copy(qw_hbm, qw_ref, load_sem.at[8])
    small_loads = [
        pltpu.make_async_copy(source, target, load_sem.at[2 + i])
        for i, (source, target) in enumerate(
            (
                (w_in_hbm, w_in_ref), (b_in_hbm, b_in_ref), (w_out_hbm, w_out_ref), (b_out_hbm, b_out_ref),
                (tinv_hbm, tinv), (tfwd_hbm, tfwd),
            )
        )
    ]
    spec_load.start()
    leg_load.start()
    weight_load.start()

    barrier = pltpu.get_barrier_semaphore()

    def greet_z(k, carry):
        other = (z + k) % ZN
        _, other_active = slot_of(other)

        @pl.when(jnp.logical_or(active, other_active))
        def _():
            pl.semaphore_signal(barrier, inc=1, device_id=device(me, other), device_id_type=MESH)

        return carry

    lax.fori_loop(1, ZN, greet_z, 0)

    @pl.when(active)
    def _():
        def greet_plane(k, carry):
            pl.semaphore_signal(barrier, inc=1, device_id=device((me + k) % PN, z), device_id_type=MESH)
            return carry

        lax.fori_loop(1, PN, greet_plane, 0)
        for load in small_loads:
            load.start()

    spec_load.wait()
    for i in range(16 * OWN_M):
        values = spec_ref[i].astype(jnp.float32)
        for b, width in enumerate((128, 128, 64)):
            spec32[b, 2 * i : 2 * i + 2, 0:width] = values[:, 128 * b : 128 * b + width]
    lane = lax.broadcasted_iota(jnp.int32, (1, WAVES), 1)
    even_lane = lane % 2 == 0
    leg_load.wait()
    pieces = [[[] for _ in range(SLOTS)] for _ in range(2)]
    for m in range(OWN_M):
        real = jnp.concatenate([spec32[b, pl.ds(2 * m, 16, stride=2 * OWN_M), :] for b in range(3)], axis=1)
        imag = jnp.concatenate([spec32[b, pl.ds(2 * m + 1, 16, stride=2 * OWN_M), :] for b in range(3)], axis=1)
        both = jnp.concatenate([real, imag], axis=0)[:, :WAVES]
        lhs = jnp.concatenate([jnp.where(even_lane, both, 0.0), jnp.where(even_lane, 0.0, both)], axis=0)
        sums = jnp.dot(lhs.astype(jnp.bfloat16), leg[m], preferred_element_type=jnp.float32)
        for h, rows in enumerate((sums[:32] + sums[32:], sums[:32] - sums[32:])):
            for s in range(SLOTS):
                cols = slice(32 * s, 32 * s + 32)
                pieces[h][s].append(jnp.concatenate([rows[8 * i : 8 * i + 8, cols] for i in range(4)], axis=1))
    for h in range(2):
        for s in range(SLOTS):
            zsend[h, s] = jnp.concatenate(pieces[h][s], axis=0).astype(jnp.bfloat16)

    @pl.when(active)
    def _():
        pl.semaphore_wait(barrier, ZN - 1 + PN - 1)

    @pl.when(jnp.logical_not(active))
    def _():
        pl.semaphore_wait(barrier, SLOTS)

    for h in range(2):

        def send_z(k, carry):
            other = (z + far_first(k)) % ZN
            s, ok = slot_of(other)

            @pl.when(ok)
            def _():
                pltpu.make_async_remote_copy(
                    zsend.at[h, s], zrecv.at[h, z], zs_sem.at[h], zr_sem.at[h],
                    device_id=device(me, other), device_id_type=MESH,
                ).start()

            return carry

        lax.fori_loop(1, ZN, send_z, 0)

    @pl.when(active)
    def _():
        for h in range(2):
            pltpu.make_async_copy(zsend.at[h, slot], zrecv.at[h, z], zr_sem.at[h]).start()
        for k in range(20, KP):
            rows32[pl.ds(k, PN, stride=KP), :] = jnp.zeros((PN, 128), jnp.float32)
        for load in small_loads:
            load.wait()

        row = lax.broadcasted_iota(jnp.int32, (128, 128), 0)
        col = lax.broadcasted_iota(jnp.int32, (128, 128), 1)
        wanted = ((row // 64) * 4 + (row % 8) // 2) * 16 + ((row // 8) % 8) * 2 + row % 2
        onehot32 = jnp.where(col == wanted, 1.0, 0.0).astype(jnp.float32)
        onehot = onehot32.astype(jnp.bfloat16)
        eye32 = jnp.where(row == col, 1.0, 0.0).astype(jnp.float32)
        w_in = jnp.dot(onehot, w_in_ref[...], preferred_element_type=jnp.float32).astype(jnp.bfloat16)
        w_out = lax.dot_general(
            w_out_ref[...], onehot, (((1,), (1,)), ((), ())), preferred_element_type=jnp.float32
        ).astype(jnp.bfloat16)
        b_col = jnp.sum(onehot32 * b_out_ref[...], axis=1, keepdims=True)
        b_out = jnp.sum(eye32 * b_col, axis=0, keepdims=True)
        b_in = b_in_ref[...]

        for h in range(2):
            pltpu.make_async_copy(zrecv.at[h], zrecv.at[h], zr_sem.at[h]).wait()
            for half in range(2):
                got = [zrecv[h, half * 8 + g].astype(jnp.float32) for g in range(8)]
                for m in range(OWN_M):
                    turned = jnp.concatenate([t[m * 8 : m * 8 + 8] for t in got], axis=0).T
                    for r in range(2):
                        q = r * 64
                        rows32[pl.ds((half * OWN_M + m) * 2 + r, PN, stride=KP), :] = jnp.concatenate(
                            [turned[q : q + 32], turned[q + 32 : q + 64]], axis=1
                        )
            psend[h] = rows32[...].reshape(PN, KP, 128).astype(jnp.bfloat16)

            def send_plane(k, carry):
                other = (me + k) % PN
                pltpu.make_async_remote_copy(
                    psend.at[h, other], precv.at[h, me], ps_sem.at[h], pr_sem.at[h],
                    device_id=device(other, z), device_id_type=MESH,
                ).start()
                return carry

            lax.fori_loop(1, PN, send_plane, 0)
            pltpu.make_async_copy(psend.at[h, me], precv.at[h, me], pr_sem.at[h]).start()

        for h in range(2):
            pltpu.make_async_copy(precv.at[h], precv.at[h], pr_sem.at[h]).wait()
            waves = precv[h].astype(jnp.float32).reshape(PN * KP, 128).astype(jnp.bfloat16)

            def columns(i, carry):
                rows = pl.ds(pl.multiple_of(i * TILE, TILE), TILE)
                grid = jnp.dot(tinv[rows, :], waves, preferred_element_type=jnp.float32).astype(jnp.bfloat16)
                hidden = jnp.dot(grid, w_in, preferred_element_type=jnp.float32) + b_in
                hidden = jax.nn.gelu(hidden).astype(jnp.bfloat16)
                value = jnp.dot(hidden, w_out, preferred_element_type=jnp.float32) + b_out
                tend[rows, :] = value.astype(jnp.bfloat16)
                return carry

            lax.fori_loop(0, NLON // TILE, columns, 0)
            coeffs = jnp.dot(tfwd[...], tend[...], preferred_element_type=jnp.float32)
            bsend[h] = coeffs.reshape(PN, KP, 128).astype(jnp.bfloat16)

            def return_plane(k, carry):
                other = (me + k) % PN
                pltpu.make_async_remote_copy(
                    bsend.at[h, other], brecv.at[h, me], bs_sem.at[h], br_sem.at[h],
                    device_id=device(other, z), device_id_type=MESH,
                ).start()
                return carry

            lax.fori_loop(1, PN, return_plane, 0)
            pltpu.make_async_copy(bsend.at[h, me], brecv.at[h, me], br_sem.at[h]).start()

        for h in range(2):
            pltpu.make_async_copy(brecv.at[h], brecv.at[h], br_sem.at[h]).wait()
            rows32[...] = brecv[h].astype(jnp.float32).reshape(PN * KP, 128)
            for half in range(2):
                turned = []
                for m in range(OWN_M):
                    blocks = []
                    for r in range(2):
                        block = rows32[pl.ds((half * OWN_M + m) * 2 + r, PN, stride=KP), :]
                        blocks += [block[:, :64], block[:, 64:]]
                    turned.append(jnp.concatenate(blocks, axis=0).T)
                for g in range(8):
                    zbsend[h, half * 8 + g] = jnp.concatenate(
                        [t[g * 8 : g * 8 + 8] for t in turned], axis=0
                    ).astype(jnp.bfloat16)

            def return_z(k, carry):
                other = (z + far_first(k)) % ZN
                pltpu.make_async_remote_copy(
                    zbsend.at[h, other], zbrecv.at[h, slot], zbs_sem.at[h], zbr_sem.at[h],
                    device_id=device(me, other), device_id_type=MESH,
                ).start()
                return carry

            lax.fori_loop(1, ZN, return_z, 0)
            pltpu.make_async_copy(zbsend.at[h, z], zbrecv.at[h, slot], zbr_sem.at[h]).start()

    for h in range(2):
        pltpu.make_async_copy(zbrecv.at[h], zbrecv.at[h], zbr_sem.at[h]).wait()

    weight_load.wait()
    weight = qw_ref[...].reshape(1, WAVES)
    got = [[zbrecv[h, s].astype(jnp.float32) for s in range(SLOTS)] for h in range(2)]
    for m in range(OWN_M):
        north, south = (
            jnp.concatenate(
                [
                    jnp.concatenate(
                        [t[m * 8 : m * 8 + 8, 32 * i : 32 * i + 32] for t in got[h]], axis=1
                    )
                    for i in range(4)
                ],
                axis=0,
            )
            for h in range(2)
        )
        lhs = jnp.concatenate([(north + south) * weight, (north - south) * weight], axis=0).astype(jnp.bfloat16)
        sums = lax.dot_general(lhs, leg[m], (((1,), (1,)), ((), ())), preferred_element_type=jnp.float32)
        result = jnp.where(even_lane, sums[:32], sums[32:])
        result = jnp.concatenate([result, jnp.zeros((32, 64), jnp.float32)], axis=1)
        for b in range(3):
            cols = slice(128 * b, 128 * b + 128)
            spec32[b, pl.ds(2 * m, 16, stride=2 * OWN_M), :] = result[:16, cols]
            spec32[b, pl.ds(2 * m + 1, 16, stride=2 * OWN_M), :] = result[16:, cols]
    for i in range(16 * OWN_M):
        for b, width in enumerate((128, 128, 64)):
            out_ref[i, :, 128 * b : 128 * b + width] = spec32[b, 2 * i : 2 * i + 2, 0:width]

    @pl.when(active)
    def _():
        for h in range(2):
            pltpu.make_async_copy(zsend.at[h, 0:9], zsend.at[h, 0:9], zs_sem.at[h]).wait()
            pltpu.make_async_copy(psend.at[h, 0:31], psend.at[h, 0:31], ps_sem.at[h]).wait()
            pltpu.make_async_copy(bsend.at[h, 0:31], bsend.at[h, 0:31], bs_sem.at[h]).wait()
            pltpu.make_async_copy(zbsend.at[h, 0:15], zbsend.at[h, 0:15], zbs_sem.at[h]).wait()

    @pl.when(jnp.logical_not(active))
    def _():
        for h in range(2):
            pltpu.make_async_copy(zsend.at[h], zsend.at[h], zs_sem.at[h]).wait()


def shards(tinv, tfwd, spectral, legendre, quad_weight, w_in, b_in, w_out, b_out):
    bf16, f32 = jnp.bfloat16, jnp.float32
    vmem, hbm = (pl.BlockSpec(memory_space=s) for s in (pltpu.VMEM, pltpu.HBM))
    out = pl.pallas_call(
        kernel,
        out_shape=jax.ShapeDtypeStruct((16 * OWN_M, 2, WAVES), f32),
        in_specs=[hbm] * 9,
        out_specs=vmem,
        scratch_shapes=[
            pltpu.VMEM((16 * OWN_M, 2, WAVES), bf16),
            pltpu.VMEM(legendre.shape, bf16),
            pltpu.VMEM(quad_weight.shape, f32),
            pltpu.VMEM(w_in.shape, bf16),
            pltpu.VMEM((1, w_in.shape[1]), f32),
            pltpu.VMEM(w_out.shape, bf16),
            pltpu.VMEM((1, w_out.shape[1]), f32),
            pltpu.VMEM((NLON, PN * KP), bf16),
            pltpu.VMEM((PN * KP, NLON), bf16),
            pltpu.VMEM((3, 32 * OWN_M, 128), f32),
            pltpu.VMEM((2, SLOTS, 8 * OWN_M, 128), bf16),
            pltpu.VMEM((2, ZN, 8 * OWN_M, 128), bf16),
            pltpu.VMEM((PN * KP, 128), f32),
            pltpu.VMEM((2, PN, KP, 128), bf16),
            pltpu.VMEM((2, PN, KP, 128), bf16),
            pltpu.VMEM((NLON, 128), bf16),
            pltpu.VMEM((2, PN, KP, 128), bf16),
            pltpu.VMEM((2, PN, KP, 128), bf16),
            pltpu.VMEM((2, ZN, 8 * OWN_M, 128), bf16),
            pltpu.VMEM((2, SLOTS, 8 * OWN_M, 128), bf16),
            pltpu.SemaphoreType.DMA((9,)),
        ]
        + [pltpu.SemaphoreType.DMA((2,))] * 8,
        compiler_params=pltpu.CompilerParams(collective_id=0, has_side_effects=True, vmem_limit_bytes=56 << 20),
        name="transform_step",
    )(
        spectral.transpose(0, 1, 3, 2, 4).reshape(16 * OWN_M, 2, WAVES), legendre, quad_weight,
        w_in, b_in.reshape(1, -1), w_out, b_out.reshape(1, -1), tinv, tfwd,
    )
    return out.reshape(8, 2, OWN_M, 2, WAVES).transpose(0, 1, 3, 2, 4)


def solution(mesh):
    tinv, tfwd = tables()
    in_specs = (P(), P(), P(None, "lev", None, "lat", None), P("lat", None, None), P(), P(), P(), P(), P())
    out_specs = P(None, "lev", None, "lat", None)
    step = jax.shard_map(shards, mesh=mesh, in_specs=in_specs, out_specs=out_specs, check_vma=False)
    return lambda *args: step(jnp.asarray(tinv), jnp.asarray(tfwd), *args)
```

```python
import functools
import math

import jax
import jax.numpy as jnp
import ml_dtypes
import numpy as np
from jax import lax
from jax.experimental import pallas as pl
from jax.experimental.pallas import tpu as pltpu
from jax.sharding import PartitionSpec as P

MESH = pl.DeviceIdType.MESH
NLON = 1280
WAVES = 320
ZN = 16
PN = 32
SLOTS = 10
OWN_M = 5
KP = 24


def tables():
    m = np.arange(WAVES, dtype=np.int64)
    x = np.arange(NLON, dtype=np.int64)
    angle = ((m[:, None] * x[None, :]) % NLON).astype(np.float32) * np.float32(2.0 * math.pi / NLON)
    cosines, sines = np.cos(angle), np.sin(angle)
    factor = np.where(m == 0, 1.0, 2.0).astype(np.float32)[:, None]
    inverse = np.stack([factor * cosines, -factor * sines], axis=1)
    forward = np.stack([cosines, -sines], axis=1) / np.float32(NLON)

    def arrange(table):
        t = table.reshape(16, 2, 2, OWN_M, 2, NLON).transpose(0, 2, 1, 3, 4, 5).reshape(PN, 4 * OWN_M, NLON)
        padded = np.zeros((PN, KP, NLON), np.float32)
        padded[:, : 4 * OWN_M] = t
        return padded.reshape(PN * KP, NLON).astype(ml_dtypes.bfloat16)

    return np.ascontiguousarray(arrange(inverse).T), arrange(forward)


def device(plane_index, z):
    return {"lat": (plane_index // 2) * 4 + (z // 8) * 2 + plane_index % 2, "lev": z % 8}


def slot_of(z):
    s = (5 * z + 7) // 8
    return s, (8 * s) // 5 == z


FAR_FIRST = (8, 7, 9, 6, 10, 5, 11, 4, 12, 3, 13, 2, 14, 1, 15)
RETURN_ORDER = (((0, 0, 6),), ((1, 0, 3), (1, 3, 6), (0, 6, 16), (1, 6, 16)))


def away(step):
    return min(step, 4 - step)


PLANE_FAR_FIRST = sorted(
    [(dy, dx, dc) for dy in range(4) for dx in range(4) for dc in range(2) if dy or dx or dc],
    key=lambda step: -(away(step[0]) + away(step[1])),
)


def plane_other(me, step):
    y, x, core = me // 8, (me // 2) % 4, me % 2
    return (((y + step[0]) % 4) * 4 + (x + step[1]) % 4) * 2 + (core + step[2]) % 2


def kernel(
    spec_hbm, leg_hbm, w_in_hbm, b_in_hbm, w_out_hbm, b_out_hbm, tinv_hbm, tfwd_hbm,
    zbrecv,
    spec_ref, leg, w_in_ref, b_in_ref, w_out_ref, b_out_ref, tinv, tfwd, spec32, zsend, zrecv, rows32, psend, precv, tend, bsend, brecv, zbsend,
    load_sem, zs_sem, zr_sem, ps_sem, pr_sem, bs_sem, br_sem, zbs_sem, zbr_sem,
):
    lat = lax.axis_index("lat")
    z = ((lat // 2) % 2) * 8 + lax.axis_index("lev")
    me = (lat // 4) * 2 + lat % 2
    slot, active = slot_of(z)

    spec_load = pltpu.make_async_copy(spec_hbm, spec_ref, load_sem.at[0])
    leg_load = pltpu.make_async_copy(leg_hbm, leg, load_sem.at[1])
    small_loads = [
        pltpu.make_async_copy(source, target, load_sem.at[2 + i])
        for i, (source, target) in enumerate(
            (
                (w_in_hbm, w_in_ref), (b_in_hbm, b_in_ref), (w_out_hbm, w_out_ref), (b_out_hbm, b_out_ref),
                (tinv_hbm, tinv), (tfwd_hbm, tfwd),
            )
        )
    ]
    spec_load.start()
    leg_load.start()

    barrier = pltpu.get_barrier_semaphore()

    for k in FAR_FIRST:
        other = (z + k) % ZN
        _, other_active = slot_of(other)

        @pl.when(jnp.logical_or(active, other_active))
        def _():
            pl.semaphore_signal(barrier, inc=1, device_id=device(me, other), device_id_type=MESH)

    @pl.when(active)
    def _():
        for step in PLANE_FAR_FIRST:
            other = plane_other(me, step)
            pl.semaphore_signal(barrier, inc=1, device_id=device(other, z), device_id_type=MESH)
        for load in small_loads:
            load.start()

    spec_load.wait()
    for i in range(16 * OWN_M):
        values = spec_ref[i].astype(jnp.float32)
        for b, width in enumerate((128, 128, 64)):
            spec32[b, 2 * i : 2 * i + 2, 0:width] = values[:, 128 * b : 128 * b + width]
    lane = lax.broadcasted_iota(jnp.int32, (1, WAVES), 1)
    even_lane = lane % 2 == 0
    leg_load.wait()
    pieces = [[[] for _ in range(SLOTS)] for _ in range(2)]
    for m in range(OWN_M):
        real = jnp.concatenate([spec32[b, pl.ds(2 * m, 16, stride=2 * OWN_M), :] for b in range(3)], axis=1)
        imag = jnp.concatenate([spec32[b, pl.ds(2 * m + 1, 16, stride=2 * OWN_M), :] for b in range(3)], axis=1)
        both = jnp.concatenate([real, imag], axis=0)[:, :WAVES]
        lhs = jnp.concatenate([jnp.where(even_lane, both, 0.0), jnp.where(even_lane, 0.0, both)], axis=0)
        sums = jnp.dot(lhs.astype(jnp.bfloat16), leg[m], preferred_element_type=jnp.float32)
        for h, rows in enumerate((sums[:32] + sums[32:], sums[:32] - sums[32:])):
            for s in range(SLOTS):
                cols = slice(32 * s, 32 * s + 32)
                pieces[h][s].append(jnp.concatenate([rows[8 * i : 8 * i + 8, cols] for i in range(4)], axis=1))
    for h in range(2):
        for s in range(SLOTS):
            zsend[h, s] = jnp.concatenate(pieces[h][s], axis=0).astype(jnp.bfloat16)

    @pl.when(active)
    def _():
        pl.semaphore_wait(barrier, ZN - 1 + PN - 1)

    @pl.when(jnp.logical_not(active))
    def _():
        pl.semaphore_wait(barrier, SLOTS)

    def wait_z(h):
        @pl.when(active)
        def _():
            pltpu.make_async_copy(zsend.at[h, 0:9], zsend.at[h, 0:9], zs_sem.at[h]).wait()

        @pl.when(jnp.logical_not(active))
        def _():
            pltpu.make_async_copy(zsend.at[h], zsend.at[h], zs_sem.at[h]).wait()

    for h in range(2):
        for k in FAR_FIRST:
            other = (z + k) % ZN
            other_slot, other_active = slot_of(other)

            @pl.when(other_active)
            def _():
                pltpu.make_async_remote_copy(
                    zsend.at[h, other_slot], zrecv.at[h, z], zs_sem.at[h], zr_sem.at[h],
                    device_id=device(me, other), device_id_type=MESH,
                ).start()

        if h == 0:
            wait_z(0)

    @pl.when(active)
    def _():
        for h in range(2):
            pltpu.make_async_copy(zsend.at[h, slot], zrecv.at[h, z], zr_sem.at[h]).start()
        for k in range(20, KP):
            rows32[pl.ds(k, PN, stride=KP), :] = jnp.zeros((PN, 128), jnp.float32)
        for load in small_loads:
            load.wait()

        row = lax.broadcasted_iota(jnp.int32, (128, 128), 0)
        col = lax.broadcasted_iota(jnp.int32, (128, 128), 1)
        wanted = ((row // 64) * 4 + (row % 8) // 2) * 16 + ((row // 8) % 8) * 2 + row % 2
        onehot32 = jnp.where(col == wanted, 1.0, 0.0).astype(jnp.float32)
        onehot = onehot32.astype(jnp.bfloat16)
        eye32 = jnp.where(row == col, 1.0, 0.0).astype(jnp.float32)
        w_in = jnp.dot(onehot, w_in_ref[...], preferred_element_type=jnp.float32).astype(jnp.bfloat16)
        w_out = lax.dot_general(
            w_out_ref[...], onehot, (((1,), (1,)), ((), ())), preferred_element_type=jnp.float32
        ).astype(jnp.bfloat16)
        b_col = jnp.sum(onehot32 * b_out_ref[...], axis=1, keepdims=True)
        b_out = jnp.sum(eye32 * b_col, axis=0, keepdims=True)
        b_in = b_in_ref[...]

        for h in range(2):
            pltpu.make_async_copy(zrecv.at[h], zrecv.at[h], zr_sem.at[h]).wait()
            for half in range(2):
                got = [zrecv[h, half * 8 + g].astype(jnp.float32) for g in range(8)]
                for m in range(OWN_M):
                    turned = jnp.concatenate([t[m * 8 : m * 8 + 8] for t in got], axis=0).T
                    for r in range(2):
                        q = r * 64
                        rows32[pl.ds((half * OWN_M + m) * 2 + r, PN, stride=KP), :] = jnp.concatenate(
                            [turned[q : q + 32], turned[q + 32 : q + 64]], axis=1
                        )
            psend[h] = rows32[...].reshape(PN, KP, 128).astype(jnp.bfloat16)

            for step in PLANE_FAR_FIRST:
                other = plane_other(me, step)
                pltpu.make_async_remote_copy(
                    psend.at[h, other], precv.at[h, me], ps_sem.at[h], pr_sem.at[h],
                    device_id=device(other, z), device_id_type=MESH,
                ).start()
            pltpu.make_async_copy(psend.at[h, me], precv.at[h, me], pr_sem.at[h]).start()

        for h in range(2):
            pltpu.make_async_copy(precv.at[h], precv.at[h], pr_sem.at[h]).wait()
            waves = precv[h].astype(jnp.float32).reshape(PN * KP, 128).astype(jnp.bfloat16)

            grid = jnp.dot(tinv[...], waves, preferred_element_type=jnp.float32).astype(jnp.bfloat16)
            hidden = jnp.dot(grid, w_in, preferred_element_type=jnp.float32) + b_in
            hidden = jax.nn.gelu(hidden).astype(jnp.bfloat16)
            value = jnp.dot(hidden, w_out, preferred_element_type=jnp.float32) + b_out
            tend[...] = value.astype(jnp.bfloat16)
            coeffs = jnp.dot(tfwd[...], tend[...], preferred_element_type=jnp.float32)
            bsend[h] = coeffs.reshape(PN, KP, 128).astype(jnp.bfloat16)

            for step in PLANE_FAR_FIRST:
                other = plane_other(me, step)
                pltpu.make_async_remote_copy(
                    bsend.at[h, other], brecv.at[h, me], bs_sem.at[h], br_sem.at[h],
                    device_id=device(other, z), device_id_type=MESH,
                ).start()
            pltpu.make_async_copy(bsend.at[h, me], brecv.at[h, me], br_sem.at[h]).start()

        def return_z(h, low, high):
            for step in FAR_FIRST:
                other = (z + step) % ZN

                @pl.when(jnp.logical_and(other >= low, other < high))
                def _():
                    pltpu.make_async_remote_copy(
                        zbsend.at[h, other], zbrecv.at[h, slot], zbs_sem.at[h], zbr_sem.at[h],
                        device_id=device(me, other), device_id_type=MESH,
                    ).start()

        for h in range(2):
            pltpu.make_async_copy(brecv.at[h], brecv.at[h], br_sem.at[h]).wait()
            rows32[...] = brecv[h].astype(jnp.float32).reshape(PN * KP, 128)
            for half in range(2):
                turned = []
                for m in range(OWN_M):
                    blocks = []
                    for r in range(2):
                        block = rows32[pl.ds((half * OWN_M + m) * 2 + r, PN, stride=KP), :]
                        blocks += [block[:, :64], block[:, 64:]]
                    turned.append(jnp.concatenate(blocks, axis=0).T)
                for g in range(8):
                    zbsend[h, half * 8 + g] = jnp.concatenate(
                        [t[g * 8 : g * 8 + 8] for t in turned], axis=0
                    ).astype(jnp.bfloat16)

            for chunk, low, high in RETURN_ORDER[h]:
                return_z(chunk, low, high)
            pltpu.make_async_copy(zbsend.at[h, z], zbrecv.at[h, slot], zbr_sem.at[h]).start()

    for h in range(2):
        pltpu.make_async_copy(zbrecv.at[h], zbrecv.at[h], zbr_sem.at[h]).wait()

    wait_z(1)

    @pl.when(active)
    def _():
        for h in range(2):
            pltpu.make_async_copy(psend.at[h, 0:31], psend.at[h, 0:31], ps_sem.at[h]).wait()
            pltpu.make_async_copy(bsend.at[h, 0:31], bsend.at[h, 0:31], bs_sem.at[h]).wait()
            pltpu.make_async_copy(zbsend.at[h, 0:15], zbsend.at[h, 0:15], zbs_sem.at[h]).wait()


def last_sums(zbrecv, leg, qw_ref, out_ref, spec32):
    even_lane = lax.broadcasted_iota(jnp.int32, (1, WAVES), 1) % 2 == 0

    weight = qw_ref[...].reshape(1, WAVES)
    got = [[zbrecv[h, s].astype(jnp.float32) for s in range(SLOTS)] for h in range(2)]
    for m in range(OWN_M):
        north, south = (
            jnp.concatenate(
                [
                    jnp.concatenate(
                        [t[m * 8 : m * 8 + 8, 32 * i : 32 * i + 32] for t in got[h]], axis=1
                    )
                    for i in range(4)
                ],
                axis=0,
            )
            for h in range(2)
        )
        lhs = jnp.concatenate([(north + south) * weight, (north - south) * weight], axis=0).astype(jnp.bfloat16)
        sums = lax.dot_general(lhs, leg[m], (((1,), (1,)), ((), ())), preferred_element_type=jnp.float32)
        result = jnp.where(even_lane, sums[:32], sums[32:])
        result = jnp.concatenate([result, jnp.zeros((32, 64), jnp.float32)], axis=1)
        for b in range(3):
            cols = slice(128 * b, 128 * b + 128)
            spec32[b, pl.ds(2 * m, 16, stride=2 * OWN_M), :] = result[:16, cols]
            spec32[b, pl.ds(2 * m + 1, 16, stride=2 * OWN_M), :] = result[16:, cols]
    for i in range(16 * OWN_M):
        for b, width in enumerate((128, 128, 64)):
            out_ref[i, :, 128 * b : 128 * b + width] = spec32[b, 2 * i : 2 * i + 2, 0:width]


def shards(tinv, tfwd, spectral, legendre, quad_weight, w_in, b_in, w_out, b_out):
    bf16, f32 = jnp.bfloat16, jnp.float32
    vmem, hbm = (pl.BlockSpec(memory_space=s) for s in (pltpu.VMEM, pltpu.HBM))
    back = pl.pallas_call(
        kernel,
        out_shape=jax.ShapeDtypeStruct((2, SLOTS, 8 * OWN_M, 128), bf16),
        in_specs=[hbm] * 8,
        out_specs=vmem,
        scratch_shapes=[
            pltpu.VMEM((16 * OWN_M, 2, WAVES), bf16),
            pltpu.VMEM(legendre.shape, bf16),
            pltpu.VMEM(w_in.shape, bf16),
            pltpu.VMEM((1, w_in.shape[1]), f32),
            pltpu.VMEM(w_out.shape, bf16),
            pltpu.VMEM((1, w_out.shape[1]), f32),
            pltpu.VMEM((NLON, PN * KP), bf16),
            pltpu.VMEM((PN * KP, NLON), bf16),
            pltpu.VMEM((3, 32 * OWN_M, 128), f32),
            pltpu.VMEM((2, SLOTS, 8 * OWN_M, 128), bf16),
            pltpu.VMEM((2, ZN, 8 * OWN_M, 128), bf16),
            pltpu.VMEM((PN * KP, 128), f32),
            pltpu.VMEM((2, PN, KP, 128), bf16),
            pltpu.VMEM((2, PN, KP, 128), bf16),
            pltpu.VMEM((NLON, 128), bf16),
            pltpu.VMEM((2, PN, KP, 128), bf16),
            pltpu.VMEM((2, PN, KP, 128), bf16),
            pltpu.VMEM((2, ZN, 8 * OWN_M, 128), bf16),
            pltpu.SemaphoreType.DMA((8,)),
        ]
        + [pltpu.SemaphoreType.DMA((2,))] * 8,
        compiler_params=pltpu.CompilerParams(collective_id=0, has_side_effects=True, vmem_limit_bytes=56 << 20),
        name="transform_step",
    )(
        spectral.transpose(0, 1, 3, 2, 4).reshape(16 * OWN_M, 2, WAVES), legendre,
        w_in, b_in.reshape(1, -1), w_out, b_out.reshape(1, -1), tinv, tfwd,
    )
    out = pl.pallas_call(
        last_sums,
        out_shape=jax.ShapeDtypeStruct((16 * OWN_M, 2, WAVES), f32),
        in_specs=[vmem] * 3,
        out_specs=vmem,
        scratch_shapes=[pltpu.VMEM((3, 32 * OWN_M, 128), f32)],
        compiler_params=pltpu.CompilerParams(vmem_limit_bytes=56 << 20),
        name="last_sums",
    )(back, legendre, quad_weight)
    return out.reshape(8, 2, OWN_M, 2, WAVES).transpose(0, 1, 3, 2, 4)


def solution(mesh):
    tinv, tfwd = tables()
    in_specs = (P(), P(), P(None, "lev", None, "lat", None), P("lat", None, None), P(), P(), P(), P(), P())
    out_specs = P(None, "lev", None, "lat", None)
    step = jax.shard_map(shards, mesh=mesh, in_specs=in_specs, out_specs=out_specs, check_vma=False)
    return lambda *args: step(jnp.asarray(tinv), jnp.asarray(tfwd), *args)
```

```python
import functools
import math

import jax
import jax.numpy as jnp
import ml_dtypes
import numpy as np
from jax import lax
from jax.experimental import pallas as pl
from jax.experimental.pallas import tpu as pltpu
from jax.sharding import PartitionSpec as P

MESH = pl.DeviceIdType.MESH
NLON = 1280
WAVES = 320
ZN = 16
PN = 32
SLOTS = 10
OWN_M = 5
KP = 24


def tables():
    m = np.arange(WAVES, dtype=np.int64)
    x = np.arange(NLON, dtype=np.int64)
    angle = ((m[:, None] * x[None, :]) % NLON).astype(np.float32) * np.float32(2.0 * math.pi / NLON)
    cosines, sines = np.cos(angle), np.sin(angle)
    factor = np.where(m == 0, 1.0, 2.0).astype(np.float32)[:, None]
    inverse = np.stack([factor * cosines, -factor * sines], axis=1)
    forward = np.stack([cosines, -sines], axis=1) / np.float32(NLON)

    def arrange(table):
        t = table.reshape(16, 2, 2, OWN_M, 2, NLON).transpose(0, 2, 1, 3, 4, 5).reshape(PN, 4 * OWN_M, NLON)
        padded = np.zeros((PN, KP, NLON), np.float32)
        padded[:, : 4 * OWN_M] = t
        return padded.reshape(PN * KP, NLON).astype(ml_dtypes.bfloat16)

    return np.ascontiguousarray(arrange(inverse).T), arrange(forward)


def device(plane_index, z):
    return {"lat": (plane_index // 2) * 4 + (z // 8) * 2 + plane_index % 2, "lev": z % 8}


def slot_of(z):
    s = (5 * z + 7) // 8
    return s, (8 * s) // 5 == z


FAR_FIRST = (8, 7, 9, 6, 10, 5, 11, 4, 12, 3, 13, 2, 14, 1, 15)
RETURN_ORDER = (((0, 0, 6),), ((1, 0, 3), (1, 3, 6), (0, 6, 16), (1, 6, 16)))


def away(step):
    return min(step, 4 - step)


PLANE_FAR_FIRST = sorted(
    [(dy, dx, dc) for dy in range(4) for dx in range(4) for dc in range(2) if dy or dx or dc],
    key=lambda step: -(away(step[0]) + away(step[1])),
)


def plane_other(me, step):
    y, x, core = me // 8, (me // 2) % 4, me % 2
    return (((y + step[0]) % 4) * 4 + (x + step[1]) % 4) * 2 + (core + step[2]) % 2


def kernel(
    spec_hbm, leg_hbm, w_in_hbm, b_in_hbm, w_out_hbm, b_out_hbm, tinv_hbm, tfwd_hbm,
    zbrecv,
    spec_ref, leg, w_in_ref, b_in_ref, w_out_ref, b_out_ref, tinv, tfwd, spec32, zsend, zrecv, rows32, psend, precv, tend, bsend, brecv, zbsend,
    load_sem, zs_sem, zr_sem, ps_sem, pr_sem, bs_sem, br_sem, zbs_sem, zbr_sem,
):
    lat = lax.axis_index("lat")
    z = ((lat // 2) % 2) * 8 + lax.axis_index("lev")
    me = (lat // 4) * 2 + lat % 2
    slot, active = slot_of(z)

    spec_load = pltpu.make_async_copy(spec_hbm, spec_ref, load_sem.at[0])
    leg_load = pltpu.make_async_copy(leg_hbm, leg, load_sem.at[1])
    small_loads = [
        pltpu.make_async_copy(source, target, load_sem.at[2 + i])
        for i, (source, target) in enumerate(
            (
                (w_in_hbm, w_in_ref), (b_in_hbm, b_in_ref), (w_out_hbm, w_out_ref), (b_out_hbm, b_out_ref),
                (tinv_hbm, tinv), (tfwd_hbm, tfwd),
            )
        )
    ]
    spec_load.start()
    leg_load.start()

    barrier = pltpu.get_barrier_semaphore()

    for k in FAR_FIRST:
        other = (z + k) % ZN
        _, other_active = slot_of(other)

        @pl.when(jnp.logical_or(active, other_active))
        def _():
            pl.semaphore_signal(barrier, inc=1, device_id=device(me, other), device_id_type=MESH)

    @pl.when(active)
    def _():
        for step in PLANE_FAR_FIRST:
            other = plane_other(me, step)
            pl.semaphore_signal(barrier, inc=1, device_id=device(other, z), device_id_type=MESH)
        for load in small_loads:
            load.start()

    spec_load.wait()
    for i in range(16 * OWN_M):
        values = spec_ref[i].astype(jnp.float32)
        for b, width in enumerate((128, 128, 64)):
            spec32[b, 2 * i : 2 * i + 2, 0:width] = values[:, 128 * b : 128 * b + width]
    lane = lax.broadcasted_iota(jnp.int32, (1, WAVES), 1)
    even_lane = lane % 2 == 0
    leg_load.wait()
    pieces = [[[] for _ in range(SLOTS)] for _ in range(2)]
    for m in range(OWN_M):
        real = jnp.concatenate([spec32[b, pl.ds(2 * m, 16, stride=2 * OWN_M), :] for b in range(3)], axis=1)
        imag = jnp.concatenate([spec32[b, pl.ds(2 * m + 1, 16, stride=2 * OWN_M), :] for b in range(3)], axis=1)
        both = jnp.concatenate([real, imag], axis=0)[:, :WAVES]
        lhs = jnp.concatenate([jnp.where(even_lane, both, 0.0), jnp.where(even_lane, 0.0, both)], axis=0)
        sums = jnp.dot(lhs.astype(jnp.bfloat16), leg[m], preferred_element_type=jnp.float32)
        for h, rows in enumerate((sums[:32] + sums[32:], sums[:32] - sums[32:])):
            for s in range(SLOTS):
                cols = slice(32 * s, 32 * s + 32)
                pieces[h][s].append(jnp.concatenate([rows[8 * i : 8 * i + 8, cols] for i in range(4)], axis=1))
    for h in range(2):
        for s in range(SLOTS):
            zsend[h, s] = jnp.concatenate(pieces[h][s], axis=0).astype(jnp.bfloat16)

    @pl.when(active)
    def _():
        pl.semaphore_wait(barrier, ZN - 1 + PN - 1)

    @pl.when(jnp.logical_not(active))
    def _():
        pl.semaphore_wait(barrier, SLOTS)

    def wait_z(h):
        @pl.when(active)
        def _():
            pltpu.make_async_copy(zsend.at[h, 0:9], zsend.at[h, 0:9], zs_sem.at[h]).wait()

        @pl.when(jnp.logical_not(active))
        def _():
            pltpu.make_async_copy(zsend.at[h], zsend.at[h], zs_sem.at[h]).wait()

    def send_z(h, low, high, inside):
        for k in FAR_FIRST:
            other = (z + k) % ZN
            other_slot, other_active = slot_of(other)
            within = jnp.logical_and(other >= low, other < high)
            within = within if inside else jnp.logical_not(within)

            @pl.when(jnp.logical_and(other_active, within))
            def _():
                pltpu.make_async_remote_copy(
                    zsend.at[h, other_slot], zrecv.at[h, z], zs_sem.at[h], zr_sem.at[h],
                    device_id=device(me, other), device_id_type=MESH,
                ).start()

    send_z(0, 0, ZN, True)
    wait_z(0)
    send_z(1, 5, 12, True)
    send_z(1, 5, 12, False)

    @pl.when(active)
    def _():
        for h in range(2):
            pltpu.make_async_copy(zsend.at[h, slot], zrecv.at[h, z], zr_sem.at[h]).start()
        for k in range(20, KP):
            rows32[pl.ds(k, PN, stride=KP), :] = jnp.zeros((PN, 128), jnp.float32)
        for load in small_loads:
            load.wait()

        row = lax.broadcasted_iota(jnp.int32, (128, 128), 0)
        col = lax.broadcasted_iota(jnp.int32, (128, 128), 1)
        wanted = ((row // 64) * 4 + (row % 8) // 2) * 16 + ((row // 8) % 8) * 2 + row % 2
        onehot32 = jnp.where(col == wanted, 1.0, 0.0).astype(jnp.float32)
        onehot = onehot32.astype(jnp.bfloat16)
        eye32 = jnp.where(row == col, 1.0, 0.0).astype(jnp.float32)
        w_in = jnp.dot(onehot, w_in_ref[...], preferred_element_type=jnp.float32).astype(jnp.bfloat16)
        w_out = lax.dot_general(
            w_out_ref[...], onehot, (((1,), (1,)), ((), ())), preferred_element_type=jnp.float32
        ).astype(jnp.bfloat16)
        b_col = jnp.sum(onehot32 * b_out_ref[...], axis=1, keepdims=True)
        b_out = jnp.sum(eye32 * b_col, axis=0, keepdims=True)
        b_in = b_in_ref[...]

        for h in range(2):
            pltpu.make_async_copy(zrecv.at[h], zrecv.at[h], zr_sem.at[h]).wait()
            for half in range(2):
                got = [zrecv[h, half * 8 + g].astype(jnp.float32) for g in range(8)]
                for m in range(OWN_M):
                    turned = jnp.concatenate([t[m * 8 : m * 8 + 8] for t in got], axis=0).T
                    for r in range(2):
                        q = r * 64
                        rows32[pl.ds((half * OWN_M + m) * 2 + r, PN, stride=KP), :] = jnp.concatenate(
                            [turned[q : q + 32], turned[q + 32 : q + 64]], axis=1
                        )
            psend[h] = rows32[...].reshape(PN, KP, 128).astype(jnp.bfloat16)

            for step in PLANE_FAR_FIRST:
                other = plane_other(me, step)
                pltpu.make_async_remote_copy(
                    psend.at[h, other], precv.at[h, me], ps_sem.at[h], pr_sem.at[h],
                    device_id=device(other, z), device_id_type=MESH,
                ).start()
            pltpu.make_async_copy(psend.at[h, me], precv.at[h, me], pr_sem.at[h]).start()

        for h in range(2):
            pltpu.make_async_copy(precv.at[h], precv.at[h], pr_sem.at[h]).wait()
            waves = precv[h].astype(jnp.float32).reshape(PN * KP, 128).astype(jnp.bfloat16)

            grid = jnp.dot(tinv[...], waves, preferred_element_type=jnp.float32).astype(jnp.bfloat16)
            hidden = jnp.dot(grid, w_in, preferred_element_type=jnp.float32) + b_in
            hidden = jax.nn.gelu(hidden).astype(jnp.bfloat16)
            value = jnp.dot(hidden, w_out, preferred_element_type=jnp.float32) + b_out
            tend[...] = value.astype(jnp.bfloat16)
            coeffs = jnp.dot(tfwd[...], tend[...], preferred_element_type=jnp.float32)
            bsend[h] = coeffs.reshape(PN, KP, 128).astype(jnp.bfloat16)

            for step in PLANE_FAR_FIRST:
                other = plane_other(me, step)
                pltpu.make_async_remote_copy(
                    bsend.at[h, other], brecv.at[h, me], bs_sem.at[h], br_sem.at[h],
                    device_id=device(other, z), device_id_type=MESH,
                ).start()
            pltpu.make_async_copy(bsend.at[h, me], brecv.at[h, me], br_sem.at[h]).start()

        def return_z(h, low, high):
            for step in FAR_FIRST:
                other = (z + step) % ZN

                @pl.when(jnp.logical_and(other >= low, other < high))
                def _():
                    pltpu.make_async_remote_copy(
                        zbsend.at[h, other], zbrecv.at[h, slot], zbs_sem.at[h], zbr_sem.at[h],
                        device_id=device(me, other), device_id_type=MESH,
                    ).start()

        for h in range(2):
            pltpu.make_async_copy(brecv.at[h], brecv.at[h], br_sem.at[h]).wait()
            rows32[...] = brecv[h].astype(jnp.float32).reshape(PN * KP, 128)
            for half in range(2):
                turned = []
                for m in range(OWN_M):
                    blocks = []
                    for r in range(2):
                        block = rows32[pl.ds((half * OWN_M + m) * 2 + r, PN, stride=KP), :]
                        blocks += [block[:, :64], block[:, 64:]]
                    turned.append(jnp.concatenate(blocks, axis=0).T)
                for g in range(8):
                    zbsend[h, half * 8 + g] = jnp.concatenate(
                        [t[g * 8 : g * 8 + 8] for t in turned], axis=0
                    ).astype(jnp.bfloat16)

            for chunk, low, high in RETURN_ORDER[h]:
                return_z(chunk, low, high)
            pltpu.make_async_copy(zbsend.at[h, z], zbrecv.at[h, slot], zbr_sem.at[h]).start()

    for h in range(2):
        pltpu.make_async_copy(zbrecv.at[h], zbrecv.at[h], zbr_sem.at[h]).wait()

    wait_z(1)

    @pl.when(active)
    def _():
        for h in range(2):
            pltpu.make_async_copy(psend.at[h, 0:31], psend.at[h, 0:31], ps_sem.at[h]).wait()
            pltpu.make_async_copy(bsend.at[h, 0:31], bsend.at[h, 0:31], bs_sem.at[h]).wait()
            pltpu.make_async_copy(zbsend.at[h, 0:15], zbsend.at[h, 0:15], zbs_sem.at[h]).wait()


def last_sums(zbrecv, leg, qw_ref, out_ref, spec32):
    even_lane = lax.broadcasted_iota(jnp.int32, (1, WAVES), 1) % 2 == 0

    weight = qw_ref[...].reshape(1, WAVES)
    got = [[zbrecv[h, s].astype(jnp.float32) for s in range(SLOTS)] for h in range(2)]
    for m in range(OWN_M):
        north, south = (
            jnp.concatenate(
                [
                    jnp.concatenate(
                        [t[m * 8 : m * 8 + 8, 32 * i : 32 * i + 32] for t in got[h]], axis=1
                    )
                    for i in range(4)
                ],
                axis=0,
            )
            for h in range(2)
        )
        lhs = jnp.concatenate([(north + south) * weight, (north - south) * weight], axis=0).astype(jnp.bfloat16)
        sums = lax.dot_general(lhs, leg[m], (((1,), (1,)), ((), ())), preferred_element_type=jnp.float32)
        result = jnp.where(even_lane, sums[:32], sums[32:])
        result = jnp.concatenate([result, jnp.zeros((32, 64), jnp.float32)], axis=1)
        for b in range(3):
            cols = slice(128 * b, 128 * b + 128)
            spec32[b, pl.ds(2 * m, 16, stride=2 * OWN_M), :] = result[:16, cols]
            spec32[b, pl.ds(2 * m + 1, 16, stride=2 * OWN_M), :] = result[16:, cols]
    for i in range(16 * OWN_M):
        for b, width in enumerate((128, 128, 64)):
            out_ref[i, :, 128 * b : 128 * b + width] = spec32[b, 2 * i : 2 * i + 2, 0:width]


def shards(tinv, tfwd, spectral, legendre, quad_weight, w_in, b_in, w_out, b_out):
    bf16, f32 = jnp.bfloat16, jnp.float32
    vmem, hbm = (pl.BlockSpec(memory_space=s) for s in (pltpu.VMEM, pltpu.HBM))
    back = pl.pallas_call(
        kernel,
        out_shape=jax.ShapeDtypeStruct((2, SLOTS, 8 * OWN_M, 128), bf16),
        in_specs=[hbm] * 8,
        out_specs=vmem,
        scratch_shapes=[
            pltpu.VMEM((16 * OWN_M, 2, WAVES), bf16),
            pltpu.VMEM(legendre.shape, bf16),
            pltpu.VMEM(w_in.shape, bf16),
            pltpu.VMEM((1, w_in.shape[1]), f32),
            pltpu.VMEM(w_out.shape, bf16),
            pltpu.VMEM((1, w_out.shape[1]), f32),
            pltpu.VMEM((NLON, PN * KP), bf16),
            pltpu.VMEM((PN * KP, NLON), bf16),
            pltpu.VMEM((3, 32 * OWN_M, 128), f32),
            pltpu.VMEM((2, SLOTS, 8 * OWN_M, 128), bf16),
            pltpu.VMEM((2, ZN, 8 * OWN_M, 128), bf16),
            pltpu.VMEM((PN * KP, 128), f32),
            pltpu.VMEM((2, PN, KP, 128), bf16),
            pltpu.VMEM((2, PN, KP, 128), bf16),
            pltpu.VMEM((NLON, 128), bf16),
            pltpu.VMEM((2, PN, KP, 128), bf16),
            pltpu.VMEM((2, PN, KP, 128), bf16),
            pltpu.VMEM((2, ZN, 8 * OWN_M, 128), bf16),
            pltpu.SemaphoreType.DMA((8,)),
        ]
        + [pltpu.SemaphoreType.DMA((2,))] * 8,
        compiler_params=pltpu.CompilerParams(collective_id=0, has_side_effects=True, vmem_limit_bytes=56 << 20),
        name="transform_step",
    )(
        spectral.transpose(0, 1, 3, 2, 4).reshape(16 * OWN_M, 2, WAVES), legendre,
        w_in, b_in.reshape(1, -1), w_out, b_out.reshape(1, -1), tinv, tfwd,
    )
    out = pl.pallas_call(
        last_sums,
        out_shape=jax.ShapeDtypeStruct((16 * OWN_M, 2, WAVES), f32),
        in_specs=[vmem] * 3,
        out_specs=vmem,
        scratch_shapes=[pltpu.VMEM((3, 32 * OWN_M, 128), f32)],
        compiler_params=pltpu.CompilerParams(vmem_limit_bytes=8 << 20),
        name="last_sums",
    )(back, legendre, quad_weight)
    return out.reshape(8, 2, OWN_M, 2, WAVES).transpose(0, 1, 3, 2, 4)


def solution(mesh):
    tinv, tfwd = tables()
    in_specs = (P(), P(), P(None, "lev", None, "lat", None), P("lat", None, None), P(), P(), P(), P(), P())
    out_specs = P(None, "lev", None, "lat", None)
    step = jax.shard_map(shards, mesh=mesh, in_specs=in_specs, out_specs=out_specs, check_vma=False)
    return lambda *args: step(jnp.asarray(tinv), jnp.asarray(tfwd), *args)
```

```python
import functools
import math

import jax
import jax.numpy as jnp
import ml_dtypes
import numpy as np
from jax import lax
from jax.experimental import pallas as pl
from jax.experimental.pallas import tpu as pltpu
from jax.sharding import PartitionSpec as P

MESH = pl.DeviceIdType.MESH
NLON = 1280
WAVES = 320
ZN = 16
PN = 32
SLOTS = 10
OWN_M = 5
KP = 24


def tables():
    m = np.arange(WAVES, dtype=np.int64)
    x = np.arange(NLON, dtype=np.int64)
    angle = ((m[:, None] * x[None, :]) % NLON).astype(np.float32) * np.float32(2.0 * math.pi / NLON)
    cosines, sines = np.cos(angle), np.sin(angle)
    factor = np.where(m == 0, 1.0, 2.0).astype(np.float32)[:, None]
    inverse = np.stack([factor * cosines, -factor * sines], axis=1)
    forward = np.stack([cosines, -sines], axis=1) / np.float32(NLON)

    def arrange(table):
        t = table.reshape(16, 2, 2, OWN_M, 2, NLON).transpose(0, 2, 1, 3, 4, 5).reshape(PN, 4 * OWN_M, NLON)
        padded = np.zeros((PN, KP, NLON), np.float32)
        padded[:, : 4 * OWN_M] = t
        return padded.reshape(PN * KP, NLON).astype(ml_dtypes.bfloat16)

    return np.ascontiguousarray(arrange(inverse).T), arrange(forward)


def device(plane_index, z):
    return {"lat": (plane_index // 2) * 4 + (z // 8) * 2 + plane_index % 2, "lev": z % 8}


def slot_of(z):
    s = (5 * z + 7) // 8
    return s, (8 * s) // 5 == z


FAR_FIRST = (8, 7, 9, 6, 10, 5, 11, 4, 12, 3, 13, 2, 14, 1, 15)
RETURN_ORDER = (((0, 0, 10),), ((1, 0, 3), (1, 3, 6), (0, 10, 16), (1, 6, 16)))


def away(step):
    return min(step, 4 - step)


PLANE_FAR_FIRST = sorted(
    [(dy, dx, dc) for dy in range(4) for dx in range(4) for dc in range(2) if dy or dx or dc],
    key=lambda step: -(away(step[0]) + away(step[1])),
)


def plane_other(me, step):
    y, x, core = me // 8, (me // 2) % 4, me % 2
    return (((y + step[0]) % 4) * 4 + (x + step[1]) % 4) * 2 + (core + step[2]) % 2


def kernel(
    spec_hbm, leg_hbm, w_in_hbm, b_in_hbm, w_out_hbm, b_out_hbm, tinv_hbm, tfwd_hbm,
    zbrecv,
    spec_ref, leg, w_in_ref, b_in_ref, w_out_ref, b_out_ref, tinv, tfwd, spec32, zsend, zrecv, rows32, psend, precv, tend, bsend, brecv, zbsend,
    load_sem, zs_sem, zr_sem, ps_sem, pr_sem, bs_sem, br_sem, zbs_sem, zbr_sem,
):
    lat = lax.axis_index("lat")
    z = ((lat // 2) % 2) * 8 + lax.axis_index("lev")
    me = (lat // 4) * 2 + lat % 2
    slot, active = slot_of(z)

    spec_load = pltpu.make_async_copy(spec_hbm, spec_ref, load_sem.at[0])
    leg_load = pltpu.make_async_copy(leg_hbm, leg, load_sem.at[1])
    small_loads = [
        pltpu.make_async_copy(source, target, load_sem.at[2 + i])
        for i, (source, target) in enumerate(
            (
                (w_in_hbm, w_in_ref), (b_in_hbm, b_in_ref), (w_out_hbm, w_out_ref), (b_out_hbm, b_out_ref),
                (tinv_hbm, tinv), (tfwd_hbm, tfwd),
            )
        )
    ]
    spec_load.start()
    leg_load.start()

    barrier = pltpu.get_barrier_semaphore()

    for k in FAR_FIRST:
        other = (z + k) % ZN
        _, other_active = slot_of(other)

        @pl.when(jnp.logical_or(active, other_active))
        def _():
            pl.semaphore_signal(barrier, inc=1, device_id=device(me, other), device_id_type=MESH)

    @pl.when(active)
    def _():
        for step in PLANE_FAR_FIRST:
            other = plane_other(me, step)
            pl.semaphore_signal(barrier, inc=1, device_id=device(other, z), device_id_type=MESH)
        for load in small_loads:
            load.start()

    spec_load.wait()
    for i in range(16 * OWN_M):
        values = spec_ref[i].astype(jnp.float32)
        for b, width in enumerate((128, 128, 64)):
            spec32[b, 2 * i : 2 * i + 2, 0:width] = values[:, 128 * b : 128 * b + width]
    lane = lax.broadcasted_iota(jnp.int32, (1, WAVES), 1)
    even_lane = lane % 2 == 0
    leg_load.wait()
    pieces = [[[] for _ in range(SLOTS)] for _ in range(2)]
    for m in range(OWN_M):
        real = jnp.concatenate([spec32[b, pl.ds(2 * m, 16, stride=2 * OWN_M), :] for b in range(3)], axis=1)
        imag = jnp.concatenate([spec32[b, pl.ds(2 * m + 1, 16, stride=2 * OWN_M), :] for b in range(3)], axis=1)
        both = jnp.concatenate([real, imag], axis=0)[:, :WAVES]
        lhs = jnp.concatenate([jnp.where(even_lane, both, 0.0), jnp.where(even_lane, 0.0, both)], axis=0)
        sums = jnp.dot(lhs.astype(jnp.bfloat16), leg[m], preferred_element_type=jnp.float32)
        for h, rows in enumerate((sums[:32] + sums[32:], sums[:32] - sums[32:])):
            for s in range(SLOTS):
                cols = slice(32 * s, 32 * s + 32)
                pieces[h][s].append(jnp.concatenate([rows[8 * i : 8 * i + 8, cols] for i in range(4)], axis=1))
    for h in range(2):
        for s in range(SLOTS):
            zsend[h, s] = jnp.concatenate(pieces[h][s], axis=0).astype(jnp.bfloat16)

    @pl.when(active)
    def _():
        pl.semaphore_wait(barrier, ZN - 1 + PN - 1)

    @pl.when(jnp.logical_not(active))
    def _():
        pl.semaphore_wait(barrier, SLOTS)

    def wait_z(h):
        @pl.when(active)
        def _():
            pltpu.make_async_copy(zsend.at[h, 0:9], zsend.at[h, 0:9], zs_sem.at[h]).wait()

        @pl.when(jnp.logical_not(active))
        def _():
            pltpu.make_async_copy(zsend.at[h], zsend.at[h], zs_sem.at[h]).wait()

    def send_z(h, low, high, inside):
        for k in FAR_FIRST:
            other = (z + k) % ZN
            other_slot, other_active = slot_of(other)
            within = jnp.logical_and(other >= low, other < high)
            within = within if inside else jnp.logical_not(within)

            @pl.when(jnp.logical_and(other_active, within))
            def _():
                pltpu.make_async_remote_copy(
                    zsend.at[h, other_slot], zrecv.at[h, z], zs_sem.at[h], zr_sem.at[h],
                    device_id=device(me, other), device_id_type=MESH,
                ).start()

    send_z(0, 0, ZN, True)
    wait_z(0)
    send_z(1, 5, 12, True)
    send_z(1, 5, 12, False)

    @pl.when(active)
    def _():
        for h in range(2):
            pltpu.make_async_copy(zsend.at[h, slot], zrecv.at[h, z], zr_sem.at[h]).start()
        for k in range(20, KP):
            rows32[pl.ds(k, PN, stride=KP), :] = jnp.zeros((PN, 128), jnp.float32)
        for load in small_loads:
            load.wait()

        row = lax.broadcasted_iota(jnp.int32, (128, 128), 0)
        col = lax.broadcasted_iota(jnp.int32, (128, 128), 1)
        wanted = ((row // 64) * 4 + (row % 8) // 2) * 16 + ((row // 8) % 8) * 2 + row % 2
        onehot32 = jnp.where(col == wanted, 1.0, 0.0).astype(jnp.float32)
        onehot = onehot32.astype(jnp.bfloat16)
        eye32 = jnp.where(row == col, 1.0, 0.0).astype(jnp.float32)
        w_in = jnp.dot(onehot, w_in_ref[...], preferred_element_type=jnp.float32).astype(jnp.bfloat16)
        w_out = lax.dot_general(
            w_out_ref[...], onehot, (((1,), (1,)), ((), ())), preferred_element_type=jnp.float32
        ).astype(jnp.bfloat16)
        b_col = jnp.sum(onehot32 * b_out_ref[...], axis=1, keepdims=True)
        b_out = jnp.sum(eye32 * b_col, axis=0, keepdims=True)
        b_in = b_in_ref[...]

        for h in range(2):
            pltpu.make_async_copy(zrecv.at[h], zrecv.at[h], zr_sem.at[h]).wait()
            for half in range(2):
                got = [zrecv[h, half * 8 + g].astype(jnp.float32) for g in range(8)]
                for m in range(OWN_M):
                    turned = jnp.concatenate([t[m * 8 : m * 8 + 8] for t in got], axis=0).T
                    for r in range(2):
                        q = r * 64
                        rows32[pl.ds((half * OWN_M + m) * 2 + r, PN, stride=KP), :] = jnp.concatenate(
                            [turned[q : q + 32], turned[q + 32 : q + 64]], axis=1
                        )
            psend[h] = rows32[...].reshape(PN, KP, 128).astype(jnp.bfloat16)

            for step in PLANE_FAR_FIRST:
                other = plane_other(me, step)
                pltpu.make_async_remote_copy(
                    psend.at[h, other], precv.at[h, me], ps_sem.at[h], pr_sem.at[h],
                    device_id=device(other, z), device_id_type=MESH,
                ).start()
            pltpu.make_async_copy(psend.at[h, me], precv.at[h, me], pr_sem.at[h]).start()

        for h in range(2):
            pltpu.make_async_copy(precv.at[h], precv.at[h], pr_sem.at[h]).wait()
            waves = precv[h].astype(jnp.float32).reshape(PN * KP, 128).astype(jnp.bfloat16)

            grid = jnp.dot(tinv[...], waves, preferred_element_type=jnp.float32).astype(jnp.bfloat16)
            hidden = jnp.dot(grid, w_in, preferred_element_type=jnp.float32) + b_in
            hidden = jax.nn.gelu(hidden).astype(jnp.bfloat16)
            value = jnp.dot(hidden, w_out, preferred_element_type=jnp.float32) + b_out
            tend[...] = value.astype(jnp.bfloat16)
            coeffs = jnp.dot(tfwd[...], tend[...], preferred_element_type=jnp.float32)
            bsend[h] = coeffs.reshape(PN, KP, 128).astype(jnp.bfloat16)

            for step in PLANE_FAR_FIRST:
                other = plane_other(me, step)
                pltpu.make_async_remote_copy(
                    bsend.at[h, other], brecv.at[h, me], bs_sem.at[h], br_sem.at[h],
                    device_id=device(other, z), device_id_type=MESH,
                ).start()
            pltpu.make_async_copy(bsend.at[h, me], brecv.at[h, me], br_sem.at[h]).start()

        def return_z(h, low, high):
            for step in FAR_FIRST:
                other = (z + step) % ZN

                @pl.when(jnp.logical_and(other >= low, other < high))
                def _():
                    pltpu.make_async_remote_copy(
                        zbsend.at[h, other], zbrecv.at[h, slot], zbs_sem.at[h], zbr_sem.at[h],
                        device_id=device(me, other), device_id_type=MESH,
                    ).start()

        for h in range(2):
            pltpu.make_async_copy(brecv.at[h], brecv.at[h], br_sem.at[h]).wait()
            rows32[...] = brecv[h].astype(jnp.float32).reshape(PN * KP, 128)
            for half in range(2):
                turned = []
                for m in range(OWN_M):
                    blocks = []
                    for r in range(2):
                        block = rows32[pl.ds((half * OWN_M + m) * 2 + r, PN, stride=KP), :]
                        blocks += [block[:, :64], block[:, 64:]]
                    turned.append(jnp.concatenate(blocks, axis=0).T)
                for g in range(8):
                    zbsend[h, half * 8 + g] = jnp.concatenate(
                        [t[g * 8 : g * 8 + 8] for t in turned], axis=0
                    ).astype(jnp.bfloat16)

            for chunk, low, high in RETURN_ORDER[h]:
                return_z(chunk, low, high)
            pltpu.make_async_copy(zbsend.at[h, z], zbrecv.at[h, slot], zbr_sem.at[h]).start()

    for h in range(2):
        pltpu.make_async_copy(zbrecv.at[h], zbrecv.at[h], zbr_sem.at[h]).wait()

    wait_z(1)

    @pl.when(active)
    def _():
        for h in range(2):
            pltpu.make_async_copy(psend.at[h, 0:31], psend.at[h, 0:31], ps_sem.at[h]).wait()
            pltpu.make_async_copy(bsend.at[h, 0:31], bsend.at[h, 0:31], bs_sem.at[h]).wait()
            pltpu.make_async_copy(zbsend.at[h, 0:15], zbsend.at[h, 0:15], zbs_sem.at[h]).wait()


def last_sums(zbrecv, leg, qw_ref, out_ref, spec32):
    even_lane = lax.broadcasted_iota(jnp.int32, (1, WAVES), 1) % 2 == 0

    weight = qw_ref[...].reshape(1, WAVES)
    got = [[zbrecv[h, s].astype(jnp.float32) for s in range(SLOTS)] for h in range(2)]
    for m in range(OWN_M):
        north, south = (
            jnp.concatenate(
                [
                    jnp.concatenate(
                        [t[m * 8 : m * 8 + 8, 32 * i : 32 * i + 32] for t in got[h]], axis=1
                    )
                    for i in range(4)
                ],
                axis=0,
            )
            for h in range(2)
        )
        lhs = jnp.concatenate([(north + south) * weight, (north - south) * weight], axis=0).astype(jnp.bfloat16)
        sums = lax.dot_general(lhs, leg[m], (((1,), (1,)), ((), ())), preferred_element_type=jnp.float32)
        result = jnp.where(even_lane, sums[:32], sums[32:])
        result = jnp.concatenate([result, jnp.zeros((32, 64), jnp.float32)], axis=1)
        for b in range(3):
            cols = slice(128 * b, 128 * b + 128)
            spec32[b, pl.ds(2 * m, 16, stride=2 * OWN_M), :] = result[:16, cols]
            spec32[b, pl.ds(2 * m + 1, 16, stride=2 * OWN_M), :] = result[16:, cols]
    for i in range(16 * OWN_M):
        for b, width in enumerate((128, 128, 64)):
            out_ref[i, :, 128 * b : 128 * b + width] = spec32[b, 2 * i : 2 * i + 2, 0:width]


def shards(tinv, tfwd, spectral, legendre, quad_weight, w_in, b_in, w_out, b_out):
    bf16, f32 = jnp.bfloat16, jnp.float32
    vmem, hbm = (pl.BlockSpec(memory_space=s) for s in (pltpu.VMEM, pltpu.HBM))
    back = pl.pallas_call(
        kernel,
        out_shape=jax.ShapeDtypeStruct((2, SLOTS, 8 * OWN_M, 128), bf16),
        in_specs=[hbm] * 8,
        out_specs=vmem,
        scratch_shapes=[
            pltpu.VMEM((16 * OWN_M, 2, WAVES), bf16),
            pltpu.VMEM(legendre.shape, bf16),
            pltpu.VMEM(w_in.shape, bf16),
            pltpu.VMEM((1, w_in.shape[1]), f32),
            pltpu.VMEM(w_out.shape, bf16),
            pltpu.VMEM((1, w_out.shape[1]), f32),
            pltpu.VMEM((NLON, PN * KP), bf16),
            pltpu.VMEM((PN * KP, NLON), bf16),
            pltpu.VMEM((3, 32 * OWN_M, 128), f32),
            pltpu.VMEM((2, SLOTS, 8 * OWN_M, 128), bf16),
            pltpu.VMEM((2, ZN, 8 * OWN_M, 128), bf16),
            pltpu.VMEM((PN * KP, 128), f32),
            pltpu.VMEM((2, PN, KP, 128), bf16),
            pltpu.VMEM((2, PN, KP, 128), bf16),
            pltpu.VMEM((NLON, 128), bf16),
            pltpu.VMEM((2, PN, KP, 128), bf16),
            pltpu.VMEM((2, PN, KP, 128), bf16),
            pltpu.VMEM((2, ZN, 8 * OWN_M, 128), bf16),
            pltpu.SemaphoreType.DMA((8,)),
        ]
        + [pltpu.SemaphoreType.DMA((2,))] * 8,
        compiler_params=pltpu.CompilerParams(collective_id=0, has_side_effects=True, vmem_limit_bytes=56 << 20),
        name="transform_step",
    )(
        spectral.transpose(0, 1, 3, 2, 4).reshape(16 * OWN_M, 2, WAVES), legendre,
        w_in, b_in.reshape(1, -1), w_out, b_out.reshape(1, -1), tinv, tfwd,
    )
    out = pl.pallas_call(
        last_sums,
        out_shape=jax.ShapeDtypeStruct((16 * OWN_M, 2, WAVES), f32),
        in_specs=[vmem] * 3,
        out_specs=vmem,
        scratch_shapes=[pltpu.VMEM((3, 32 * OWN_M, 128), f32)],
        compiler_params=pltpu.CompilerParams(vmem_limit_bytes=8 << 20),
        name="last_sums",
    )(back, legendre, quad_weight)
    return out.reshape(8, 2, OWN_M, 2, WAVES).transpose(0, 1, 3, 2, 4)


def solution(mesh):
    tinv, tfwd = tables()
    in_specs = (P(), P(), P(None, "lev", None, "lat", None), P("lat", None, None), P(), P(), P(), P(), P())
    out_specs = P(None, "lev", None, "lat", None)
    step = jax.shard_map(shards, mesh=mesh, in_specs=in_specs, out_specs=out_specs, check_vma=False)
    return lambda *args: step(jnp.asarray(tinv), jnp.asarray(tfwd), *args)
```

```python
import functools
import math

import jax
import jax.numpy as jnp
import ml_dtypes
import numpy as np
from jax import lax
from jax.experimental import pallas as pl
from jax.experimental.pallas import tpu as pltpu
from jax.sharding import PartitionSpec as P

MESH = pl.DeviceIdType.MESH
NLON = 1280
WAVES = 320
ZN = 16
PN = 32
SLOTS = 10
OWN_M = 5
KP = 24


def tables():
    m = np.arange(WAVES, dtype=np.int64)
    x = np.arange(NLON, dtype=np.int64)
    angle = ((m[:, None] * x[None, :]) % NLON).astype(np.float32) * np.float32(2.0 * math.pi / NLON)
    cosines, sines = np.cos(angle), np.sin(angle)
    factor = np.where(m == 0, 1.0, 2.0).astype(np.float32)[:, None]
    inverse = np.stack([factor * cosines, -factor * sines], axis=1)
    forward = np.stack([cosines, -sines], axis=1) / np.float32(NLON)

    def arrange(table):
        t = table.reshape(16, 2, 2, OWN_M, 2, NLON).transpose(0, 2, 1, 3, 4, 5).reshape(PN, 4 * OWN_M, NLON)
        padded = np.zeros((PN, KP, NLON), np.float32)
        padded[:, : 4 * OWN_M] = t
        return padded.reshape(PN * KP, NLON).astype(ml_dtypes.bfloat16)

    return np.ascontiguousarray(arrange(inverse).T), arrange(forward)


def device(plane_index, z):
    return {"lat": (plane_index // 2) * 4 + (z // 8) * 2 + plane_index % 2, "lev": z % 8}


def slot_of(z):
    s = (5 * z + 7) // 8
    return s, (8 * s) // 5 == z


FAR_FIRST = (8, 7, 9, 6, 10, 5, 11, 4, 12, 3, 13, 2, 14, 1, 15)
RETURN_ORDER = (((0, 0, 10),), ((1, 0, 3), (1, 3, 6), (0, 10, 16), (1, 6, 16)))


def away(step):
    return min(step, 4 - step)


PLANE_FAR_FIRST = sorted(
    [(dy, dx, dc) for dy in range(4) for dx in range(4) for dc in range(2) if dy or dx or dc],
    key=lambda step: -(away(step[0]) + away(step[1])),
)


def plane_other(me, step):
    y, x, core = me // 8, (me // 2) % 4, me % 2
    return (((y + step[0]) % 4) * 4 + (x + step[1]) % 4) * 2 + (core + step[2]) % 2


def kernel(
    spec_hbm, leg_hbm, w_in_hbm, b_in_hbm, w_out_hbm, b_out_hbm, tinv_hbm, tfwd_hbm,
    zbrecv,
    spec_ref, leg, w_in_ref, b_in_ref, w_out_ref, b_out_ref, tinv, tfwd, spec32, zsend, zrecv, rows32, psend, precv, tend, bsend, brecv, zbsend,
    load_sem, zs_sem, zr_sem, ps_sem, pr_sem, bs_sem, br_sem, zbs_sem, zbr_sem,
):
    lat = lax.axis_index("lat")
    z = ((lat // 2) % 2) * 8 + lax.axis_index("lev")
    me = (lat // 4) * 2 + lat % 2
    slot, active = slot_of(z)

    spec_load = pltpu.make_async_copy(spec_hbm, spec_ref, load_sem.at[0])
    leg_load = pltpu.make_async_copy(leg_hbm, leg, load_sem.at[1])
    small_loads = [
        pltpu.make_async_copy(source, target, load_sem.at[2 + i])
        for i, (source, target) in enumerate(
            (
                (w_in_hbm, w_in_ref), (b_in_hbm, b_in_ref), (w_out_hbm, w_out_ref), (b_out_hbm, b_out_ref),
                (tinv_hbm, tinv), (tfwd_hbm, tfwd),
            )
        )
    ]
    spec_load.start()
    leg_load.start()

    barrier = pltpu.get_barrier_semaphore()

    for k in FAR_FIRST:
        other = (z + k) % ZN
        _, other_active = slot_of(other)

        @pl.when(jnp.logical_or(active, other_active))
        def _():
            pl.semaphore_signal(barrier, inc=1, device_id=device(me, other), device_id_type=MESH)

    @pl.when(active)
    def _():
        for step in PLANE_FAR_FIRST:
            other = plane_other(me, step)
            pl.semaphore_signal(barrier, inc=1, device_id=device(other, z), device_id_type=MESH)
        for load in small_loads:
            load.start()

    spec_load.wait()
    for i in range(16 * OWN_M):
        values = spec_ref[i].astype(jnp.float32)
        for b, width in enumerate((128, 128, 64)):
            spec32[b, 2 * i : 2 * i + 2, 0:width] = values[:, 128 * b : 128 * b + width]
    lane = lax.broadcasted_iota(jnp.int32, (1, WAVES), 1)
    even_lane = lane % 2 == 0
    leg_load.wait()
    pieces = [[[] for _ in range(SLOTS)] for _ in range(2)]
    for m in range(OWN_M):
        real = jnp.concatenate([spec32[b, pl.ds(2 * m, 16, stride=2 * OWN_M), :] for b in range(3)], axis=1)
        imag = jnp.concatenate([spec32[b, pl.ds(2 * m + 1, 16, stride=2 * OWN_M), :] for b in range(3)], axis=1)
        both = jnp.concatenate([real, imag], axis=0)[:, :WAVES]
        lhs = jnp.concatenate([jnp.where(even_lane, both, 0.0), jnp.where(even_lane, 0.0, both)], axis=0)
        sums = jnp.dot(lhs.astype(jnp.bfloat16), leg[m], preferred_element_type=jnp.float32)
        for h, rows in enumerate((sums[:32] + sums[32:], sums[:32] - sums[32:])):
            for s in range(SLOTS):
                cols = slice(32 * s, 32 * s + 32)
                pieces[h][s].append(jnp.concatenate([rows[8 * i : 8 * i + 8, cols] for i in range(4)], axis=1))
    for h in range(2):
        for s in range(SLOTS):
            zsend[h, s] = jnp.concatenate(pieces[h][s], axis=0).astype(jnp.bfloat16)

    @pl.when(active)
    def _():
        pl.semaphore_wait(barrier, ZN - 1 + PN - 1)

    @pl.when(jnp.logical_not(active))
    def _():
        pl.semaphore_wait(barrier, SLOTS)

    def wait_z(h):
        @pl.when(active)
        def _():
            pltpu.make_async_copy(zsend.at[h, 0:9], zsend.at[h, 0:9], zs_sem.at[h]).wait()

        @pl.when(jnp.logical_not(active))
        def _():
            pltpu.make_async_copy(zsend.at[h], zsend.at[h], zs_sem.at[h]).wait()

    def send_z(h, low, high, inside):
        for k in FAR_FIRST:
            other = (z + k) % ZN
            other_slot, other_active = slot_of(other)
            within = jnp.logical_and(other >= low, other < high)
            within = within if inside else jnp.logical_not(within)

            @pl.when(jnp.logical_and(other_active, within))
            def _():
                pltpu.make_async_remote_copy(
                    zsend.at[h, other_slot], zrecv.at[h, z], zs_sem.at[h], zr_sem.at[h],
                    device_id=device(me, other), device_id_type=MESH,
                ).start()

    send_z(0, 0, ZN, True)
    wait_z(0)
    send_z(1, 5, 12, True)
    send_z(1, 5, 12, False)

    @pl.when(active)
    def _():
        for h in range(2):
            pltpu.make_async_copy(zsend.at[h, slot], zrecv.at[h, z], zr_sem.at[h]).start()
        for k in range(20, KP):
            rows32[pl.ds(k, PN, stride=KP), :] = jnp.zeros((PN, 128), jnp.float32)
        for load in small_loads:
            load.wait()

        row = lax.broadcasted_iota(jnp.int32, (128, 128), 0)
        col = lax.broadcasted_iota(jnp.int32, (128, 128), 1)
        wanted = ((row // 64) * 4 + (row % 8) // 2) * 16 + ((row // 8) % 8) * 2 + row % 2
        onehot32 = jnp.where(col == wanted, 1.0, 0.0).astype(jnp.float32)
        onehot = onehot32.astype(jnp.bfloat16)
        eye32 = jnp.where(row == col, 1.0, 0.0).astype(jnp.float32)
        w_in = jnp.dot(onehot, w_in_ref[...], preferred_element_type=jnp.float32).astype(jnp.bfloat16)
        w_out = lax.dot_general(
            w_out_ref[...], onehot, (((1,), (1,)), ((), ())), preferred_element_type=jnp.float32
        ).astype(jnp.bfloat16)
        b_col = jnp.sum(onehot32 * b_out_ref[...], axis=1, keepdims=True)
        b_out = jnp.sum(eye32 * b_col, axis=0, keepdims=True)
        b_in = b_in_ref[...]

        for h in range(2):
            pltpu.make_async_copy(zrecv.at[h], zrecv.at[h], zr_sem.at[h]).wait()
            for half in range(2):
                got = [zrecv[h, half * 8 + g].astype(jnp.float32) for g in range(8)]
                for m in range(OWN_M):
                    turned = jnp.concatenate([t[m * 8 : m * 8 + 8] for t in got], axis=0).T
                    for r in range(2):
                        q = r * 64
                        rows32[pl.ds((half * OWN_M + m) * 2 + r, PN, stride=KP), :] = jnp.concatenate(
                            [turned[q : q + 32], turned[q + 32 : q + 64]], axis=1
                        )
            psend[h] = rows32[...].reshape(PN, KP, 128).astype(jnp.bfloat16)

            for step in PLANE_FAR_FIRST:
                other = plane_other(me, step)
                pltpu.make_async_remote_copy(
                    psend.at[h, other], precv.at[h, me], ps_sem.at[h], pr_sem.at[h],
                    device_id=device(other, z), device_id_type=MESH,
                ).start()
            pltpu.make_async_copy(psend.at[h, me], precv.at[h, me], pr_sem.at[h]).start()

        for h in range(2):
            pltpu.make_async_copy(precv.at[h], precv.at[h], pr_sem.at[h]).wait()
            waves = precv[h].astype(jnp.float32).reshape(PN * KP, 128).astype(jnp.bfloat16)

            grid = jnp.dot(tinv[...], waves, preferred_element_type=jnp.float32).astype(jnp.bfloat16)
            hidden = jnp.dot(grid, w_in, preferred_element_type=jnp.float32) + b_in
            hidden = jax.nn.gelu(hidden).astype(jnp.bfloat16)
            value = jnp.dot(hidden, w_out, preferred_element_type=jnp.float32) + b_out
            tend[...] = value.astype(jnp.bfloat16)
            coeffs = jnp.dot(tfwd[...], tend[...], preferred_element_type=jnp.float32)
            bsend[h] = coeffs.reshape(PN, KP, 128).astype(jnp.bfloat16)

            for step in PLANE_FAR_FIRST:
                other = plane_other(me, step)
                pltpu.make_async_remote_copy(
                    bsend.at[h, other], brecv.at[h, me], bs_sem.at[h], br_sem.at[h],
                    device_id=device(other, z), device_id_type=MESH,
                ).start()
            pltpu.make_async_copy(bsend.at[h, me], brecv.at[h, me], br_sem.at[h]).start()

        def return_z(h, low, high):
            for other in range(low, high):

                @pl.when(other != z)
                def _():
                    pltpu.make_async_remote_copy(
                        zbsend.at[h, other], zbrecv.at[h, slot], zbs_sem.at[h], zbr_sem.at[h],
                        device_id=device(me, other), device_id_type=MESH,
                    ).start()

        for h in range(2):
            pltpu.make_async_copy(brecv.at[h], brecv.at[h], br_sem.at[h]).wait()
            rows32[...] = brecv[h].astype(jnp.float32).reshape(PN * KP, 128)
            for half in range(2):
                turned = []
                for m in range(OWN_M):
                    blocks = []
                    for r in range(2):
                        block = rows32[pl.ds((half * OWN_M + m) * 2 + r, PN, stride=KP), :]
                        blocks += [block[:, :64], block[:, 64:]]
                    turned.append(jnp.concatenate(blocks, axis=0).T)
                for g in range(8):
                    zbsend[h, half * 8 + g] = jnp.concatenate(
                        [t[g * 8 : g * 8 + 8] for t in turned], axis=0
                    ).astype(jnp.bfloat16)

            for chunk, low, high in RETURN_ORDER[h]:
                return_z(chunk, low, high)
            pltpu.make_async_copy(zbsend.at[h, z], zbrecv.at[h, slot], zbr_sem.at[h]).start()

    for h in range(2):
        pltpu.make_async_copy(zbrecv.at[h], zbrecv.at[h], zbr_sem.at[h]).wait()

    wait_z(1)

    @pl.when(active)
    def _():
        for h in range(2):
            pltpu.make_async_copy(psend.at[h, 0:31], psend.at[h, 0:31], ps_sem.at[h]).wait()
            pltpu.make_async_copy(bsend.at[h, 0:31], bsend.at[h, 0:31], bs_sem.at[h]).wait()
            pltpu.make_async_copy(zbsend.at[h, 0:15], zbsend.at[h, 0:15], zbs_sem.at[h]).wait()


def last_sums(zbrecv, leg, qw_ref, out_ref, spec32):
    even_lane = lax.broadcasted_iota(jnp.int32, (1, WAVES), 1) % 2 == 0

    weight = qw_ref[...].reshape(1, WAVES)
    got = [[zbrecv[h, s].astype(jnp.float32) for s in range(SLOTS)] for h in range(2)]
    for m in range(OWN_M):
        north, south = (
            jnp.concatenate(
                [
                    jnp.concatenate(
                        [t[m * 8 : m * 8 + 8, 32 * i : 32 * i + 32] for t in got[h]], axis=1
                    )
                    for i in range(4)
                ],
                axis=0,
            )
            for h in range(2)
        )
        lhs = jnp.concatenate([(north + south) * weight, (north - south) * weight], axis=0).astype(jnp.bfloat16)
        sums = lax.dot_general(lhs, leg[m], (((1,), (1,)), ((), ())), preferred_element_type=jnp.float32)
        result = jnp.where(even_lane, sums[:32], sums[32:])
        result = jnp.concatenate([result, jnp.zeros((32, 64), jnp.float32)], axis=1)
        for b in range(3):
            cols = slice(128 * b, 128 * b + 128)
            spec32[b, pl.ds(2 * m, 16, stride=2 * OWN_M), :] = result[:16, cols]
            spec32[b, pl.ds(2 * m + 1, 16, stride=2 * OWN_M), :] = result[16:, cols]
    for i in range(16 * OWN_M):
        for b, width in enumerate((128, 128, 64)):
            out_ref[i, :, 128 * b : 128 * b + width] = spec32[b, 2 * i : 2 * i + 2, 0:width]


def shards(tinv, tfwd, spectral, legendre, quad_weight, w_in, b_in, w_out, b_out):
    bf16, f32 = jnp.bfloat16, jnp.float32
    vmem, hbm = (pl.BlockSpec(memory_space=s) for s in (pltpu.VMEM, pltpu.HBM))
    back = pl.pallas_call(
        kernel,
        out_shape=jax.ShapeDtypeStruct((2, SLOTS, 8 * OWN_M, 128), bf16),
        in_specs=[hbm] * 8,
        out_specs=vmem,
        scratch_shapes=[
            pltpu.VMEM((16 * OWN_M, 2, WAVES), bf16),
            pltpu.VMEM(legendre.shape, bf16),
            pltpu.VMEM(w_in.shape, bf16),
            pltpu.VMEM((1, w_in.shape[1]), f32),
            pltpu.VMEM(w_out.shape, bf16),
            pltpu.VMEM((1, w_out.shape[1]), f32),
            pltpu.VMEM((NLON, PN * KP), bf16),
            pltpu.VMEM((PN * KP, NLON), bf16),
            pltpu.VMEM((3, 32 * OWN_M, 128), f32),
            pltpu.VMEM((2, SLOTS, 8 * OWN_M, 128), bf16),
            pltpu.VMEM((2, ZN, 8 * OWN_M, 128), bf16),
            pltpu.VMEM((PN * KP, 128), f32),
            pltpu.VMEM((2, PN, KP, 128), bf16),
            pltpu.VMEM((2, PN, KP, 128), bf16),
            pltpu.VMEM((NLON, 128), bf16),
            pltpu.VMEM((2, PN, KP, 128), bf16),
            pltpu.VMEM((2, PN, KP, 128), bf16),
            pltpu.VMEM((2, ZN, 8 * OWN_M, 128), bf16),
            pltpu.SemaphoreType.DMA((8,)),
        ]
        + [pltpu.SemaphoreType.DMA((2,))] * 8,
        compiler_params=pltpu.CompilerParams(collective_id=0, has_side_effects=True, vmem_limit_bytes=56 << 20),
        name="transform_step",
    )(
        spectral.transpose(0, 1, 3, 2, 4).reshape(16 * OWN_M, 2, WAVES), legendre,
        w_in, b_in.reshape(1, -1), w_out, b_out.reshape(1, -1), tinv, tfwd,
    )
    out = pl.pallas_call(
        last_sums,
        out_shape=jax.ShapeDtypeStruct((16 * OWN_M, 2, WAVES), f32),
        in_specs=[vmem] * 3,
        out_specs=vmem,
        scratch_shapes=[pltpu.VMEM((3, 32 * OWN_M, 128), f32)],
        compiler_params=pltpu.CompilerParams(vmem_limit_bytes=8 << 20),
        name="last_sums",
    )(back, legendre, quad_weight)
    return out.reshape(8, 2, OWN_M, 2, WAVES).transpose(0, 1, 3, 2, 4)


def solution(mesh):
    tinv, tfwd = tables()
    in_specs = (P(), P(), P(None, "lev", None, "lat", None), P("lat", None, None), P(), P(), P(), P(), P())
    out_specs = P(None, "lev", None, "lat", None)
    step = jax.shard_map(shards, mesh=mesh, in_specs=in_specs, out_specs=out_specs, check_vma=False)
    return lambda *args: step(jnp.asarray(tinv), jnp.asarray(tfwd), *args)
```
